256 devices in a mesh: expert: 64 (over z, x_lo, y), replica: 4 (over x_hi, core).
Axes of the slice: x: 4 (x_hi: 2, x_lo: 2; x = x_hi * 2 + x_lo), y: 4, z: 8, core: 2. Of those that a mesh axis runs over, the one named last changes fastest.
Arguments:
- mid_acts: bfloat16 [32768, 1024], P(('expert', 'replica')), may hold values from -6 to 6
- out_grad: bfloat16 [32768, 1024], P(('expert', 'replica')), may hold values from -6 to 6
- queries: bfloat16 [32768, 1024], P(('expert', 'replica')), may hold values from -45 to 45
- key_rows: bfloat16 [32768, 1024], P(('expert', 'replica')), may hold values from -6 to 6
- value_head_rows: bfloat16 [32768, 1024], P(('expert', 'replica')), may hold values from -6 to 6
- seq_lengths: int32 [256], P(('expert', 'replica')), may hold values from 32 to 128
- expert_ids: int32 [32768, 2], P(('expert', 'replica')), may hold values from 0 to 63, all different within a row
- gate_probs: bfloat16 [32768, 2], P(('expert', 'replica')), may hold values from 0.049804688 to 0.94921875
- wide_in: bfloat16 [64, 1024, 4096], P('expert', None, 'replica'), may hold values from -0.1875 to 0.1875
- wide_out: bfloat16 [64, 4096, 1024], P('expert', 'replica'), may hold values from -0.09375 to 0.09375
- attn_proj: bfloat16 [1024, 1024], replicated, may hold values from -0.1875 to 0.1875
Outputs:
- grad_mid: bfloat16 [32768, 1024], P(('expert', 'replica'))
- grad_queries: bfloat16 [32768, 1024], P(('expert', 'replica'))
- grad_keys: bfloat16 [32768, 1024], P(('expert', 'replica'))
- grad_values: bfloat16 [32768, 1024], P(('expert', 'replica'))
- grad_gates: float32 [32768, 2], P(('expert', 'replica'))
- grad_wide_in: bfloat16 [64, 1024, 4096], P('expert', None, 'replica')
- grad_wide_out: bfloat16 [64, 4096, 1024], P('expert', 'replica')
- grad_proj: bfloat16 [1024, 1024], P('expert', 'replica')
The draws below stay inside these ranges and needn't reach their ends.
Inputs may be any that keep to these rules, and one draw needn't show every extreme that they name: `expert_ids`: each token names two different experts.
All inputs are finite; a program needn't handle non-finite values.
Results may differ from the reference program's by a relative error of at most 0.015.
Values may be sent and summed in bfloat16 or wider, within the bound.
A program may use at most 192 MiB of HBM per device.

```python
import math
import jax
import jax.numpy as jnp
from jax import lax

D = 1024
HEAD_SIZE = 64
FF = 4096
SEQ = 128
TOK_DEV = 128
EXPERTS = 64
CAP = 5
TOKENS = 32768
SEQS = 256


def draw_queries(key, part):
    key = jax.random.fold_in(key, 11)
    return jax.random.normal(key, (TOKENS, D), jnp.float32).astype(jnp.bfloat16)


def draw_key_rows(key, part):
    key = jax.random.fold_in(key, 12)
    return jnp.clip(jax.random.normal(key, (TOKENS, D), jnp.float32), -6.0, 6.0).astype(jnp.bfloat16)


def draw_seq_lengths(key, part):
    key = jax.random.fold_in(key, 13)
    values = jax.random.randint(key, (SEQS,), SEQ // 4, SEQ + 1)
    return values.at[0].set(SEQ).at[1].set(SEQ // 4).astype(jnp.int32)


def steps_of(own_key, shape, shards, smallest, largest):
    factor_of, own = 1.0, jax.random.fold_in(own_key, 6)
    for position, blocks in shards:
        heights = jnp.exp(jax.random.uniform(jax.random.fold_in(own, position), (blocks,), jnp.float32, smallest / len(shards), largest / len(shards)))
        factor_of = factor_of * jnp.repeat(heights, shape[position] // blocks).reshape([-1 if axis == position else 1 for axis in range(len(shape))])
    return factor_of


def distinct(rng, rows, number_of, top, lift):
    order = jax.random.permutation(jax.random.fold_in(rng, 1), number_of)
    favour = order
    for power in range(3):
        favour = favour * favour // number_of
    favour = favour * lift // number_of
    lots = jax.random.randint(jax.random.fold_in(rng, 2), (rows, number_of), 0, 4096) + favour
    sure = jax.random.permutation(jax.random.fold_in(rng, 3), rows)[jnp.arange(number_of) % rows]
    lots = jnp.where(jnp.arange(rows)[:, None] == sure[None, :], 1 << 14, lots)
    priority = lots * number_of + jnp.arange(number_of)
    return lax.top_k(priority.astype(jnp.int32), top)[1].astype(jnp.int32)


def centred(stream_key, dims, spread, reach, cuts=(), kind=jnp.bfloat16):
    entries = spread * jax.random.normal(stream_key, dims, jnp.float32)
    if cuts:
        entries = entries * steps_of(stream_key, dims, cuts, -0.22, 0.18)
    return jnp.clip(entries, -reach, reach).astype(kind)


def setup_inputs(seed: int = 0) -> dict:
    key_of = jax.random.split(jax.random.key(seed), 12)
    return {
        "mid_acts": centred(key_of[0], (TOKENS, D), 1.0, 6.0, ((0, 256),)),
        "out_grad": centred(key_of[1], (TOKENS, D), 1.0, 6.0, ((0, 256),)),
        "queries": draw_queries(jax.random.fold_in(key_of[11], 71), 0),
        "key_rows": draw_key_rows(jax.random.fold_in(key_of[11], 71), 0),
        "value_head_rows": centred(key_of[4], (TOKENS, D), 1.0, 6.0, ((0, 256),)),
        "seq_lengths": draw_seq_lengths(jax.random.fold_in(key_of[11], 71), 0),
        "expert_ids": distinct(key_of[6], TOKENS, EXPERTS, 2, 256),
        "gate_probs": jnp.clip(0.049804688 + 0.89941406 * jax.random.uniform(key_of[7], (TOKENS, 2), jnp.float32) ** steps_of(key_of[7], (TOKENS, 2), ((0, 256),), -0.2, 0.2), 0.049804688, 0.94921875).astype(jnp.bfloat16),
        "wide_in": centred(key_of[8], (EXPERTS, D, FF), D ** -0.5, 0.1875, ((0, 64), (2, 4))),
        "wide_out": centred(key_of[9], (EXPERTS, FF, D), FF ** -0.5, 0.09375, ((0, 64), (1, 4))),
        "attn_proj": centred(key_of[10], (D, D), D ** -0.5, 0.1875),
    }


GELU_C = 0.7978845608028654
GELU_A = 0.044715

def gelu_tanh(pre):
    return 0.5 * pre * (1.0 + jnp.tanh(GELU_C * (pre + GELU_A * pre * pre * pre)))

def gelu_slope(pre):
    inner = jnp.tanh(GELU_C * (pre + GELU_A * pre * pre * pre))
    return 0.5 * (1.0 + inner) + 0.5 * pre * (1.0 - inner * inner) * GELU_C * (1.0 + 3.0 * GELU_A * pre * pre)

def group_slots(choices, experts, capacity):
    count = choices.shape[0]
    order = jnp.concatenate([choices[:, 0], choices[:, 1]])
    onehot = (order[:, None] == jnp.arange(experts, dtype=jnp.int32)[None, :]).astype(jnp.int32)
    before = jnp.cumsum(onehot, axis=0) - onehot
    place = lax.optimization_barrier(jnp.sum(before * onehot, axis=1))
    place = jnp.where(place < capacity, place, -1).astype(jnp.int32)
    return jnp.stack([place[:count], place[count:]], axis=1)

def sequence_backward(queries, key_rows, value_head_rows, d_heads, length):
    sequence_extent = queries.shape[0]
    head_split_rows = queries.shape[1] // HEAD_SIZE
    scale = 1.0 / math.sqrt(HEAD_SIZE)
    qmat = queries.reshape(sequence_extent, head_split_rows, HEAD_SIZE).astype(jnp.float32)
    kmat = key_rows.reshape(sequence_extent, head_split_rows, HEAD_SIZE).astype(jnp.float32)
    value_matrix = value_head_rows.reshape(sequence_extent, head_split_rows, HEAD_SIZE).astype(jnp.float32)
    grad_value_matrix = d_heads.reshape(sequence_extent, head_split_rows, HEAD_SIZE).astype(jnp.float32)
    scores = jnp.einsum('mnw,onw->nmo', qmat, kmat) * scale
    live = jnp.arange(sequence_extent, dtype=jnp.int32) < length
    scores = jnp.where(live[None, None, :], scores, -1000000000.0)
    top = lax.optimization_barrier(jnp.max(scores, axis=-1, keepdims=True))
    expo = jnp.exp(scores - top)
    probs = expo / lax.optimization_barrier(jnp.sum(expo, axis=-1, keepdims=True))
    batched_probabilities = lax.optimization_barrier(probs.astype(jnp.bfloat16)).astype(jnp.float32)
    attention_mixture = jnp.einsum('nea,anx->enx', batched_probabilities, value_matrix).astype(jnp.bfloat16).reshape(sequence_extent, head_split_rows * HEAD_SIZE)
    grad_probabilities = jnp.einsum('mnw,onw->nmo', grad_value_matrix, value_matrix)
    grad_v = jnp.einsum('hqk,qhd->khd', batched_probabilities, grad_value_matrix).astype(jnp.bfloat16).reshape(sequence_extent, head_split_rows * HEAD_SIZE)
    inner = lax.optimization_barrier(jnp.sum(grad_probabilities * probs, axis=-1, keepdims=True))
    dscore = lax.optimization_barrier((probs * (grad_probabilities - inner)).astype(jnp.bfloat16)).astype(jnp.float32)
    grad_q = (jnp.einsum('nea,anx->enx', dscore, kmat) * scale).astype(jnp.bfloat16).reshape(sequence_extent, head_split_rows * HEAD_SIZE)
    grad_k = (jnp.einsum('hqk,qhd->khd', dscore, qmat) * scale).astype(jnp.bfloat16).reshape(sequence_extent, head_split_rows * HEAD_SIZE)
    return (grad_q, grad_k, grad_v, attention_mixture)

def reference(mid_acts, out_grad, queries, key_rows, value_head_rows, seq_lengths, expert_ids, gate_probs, wide_in, wide_out, attn_proj):
    groups = TOKENS // TOK_DEV
    slots = jax.vmap(lambda picks: group_slots(picks, EXPERTS, CAP))(expert_ids.reshape(groups, TOK_DEV, 2)).reshape(TOKENS, 2)
    anchor = (jnp.arange(TOKENS, dtype=jnp.int32) // TOK_DEV)[:, None]
    spare = groups * CAP

    def per_expert(carry, expert):
        moe_dx, grad_gates = carry
        valid = (expert_ids == expert) & (slots >= 0)
        target = jnp.where(valid, anchor * CAP + slots, spare).astype(jnp.int32)
        xs_rows = jnp.zeros((spare + 1, D), jnp.bfloat16).at[target[:, 0]].set(mid_acts).at[target[:, 1]].set(mid_acts)[:spare]
        gs_rows = jnp.zeros((spare + 1, D), jnp.bfloat16).at[target[:, 0]].set(out_grad).at[target[:, 1]].set(out_grad)[:spare]
        gate_col = jnp.zeros((spare + 1,), jnp.bfloat16).at[target[:, 0]].set(gate_probs[:, 0]).at[target[:, 1]].set(gate_probs[:, 1])[:spare]
        w_in = wide_in[expert]
        w_out = wide_out[expert]
        pre = jnp.dot(xs_rows, w_in, preferred_element_type=jnp.float32)
        act = gelu_tanh(pre).astype(jnp.bfloat16)
        scaled = (gate_col.astype(jnp.float32)[:, None] * gs_rows.astype(jnp.float32)).astype(jnp.bfloat16)
        d_act = jnp.dot(scaled, w_out.T, preferred_element_type=jnp.float32)
        d_pre = (d_act * gelu_slope(pre)).astype(jnp.bfloat16)
        grad_in = jnp.dot(xs_rows.T, d_pre, preferred_element_type=jnp.float32).astype(jnp.bfloat16)
        grad_out = jnp.dot(act.T, scaled, preferred_element_type=jnp.float32).astype(jnp.bfloat16)
        slot_dx = jnp.dot(d_pre, w_in.T, preferred_element_type=jnp.float32)
        slot_out = jnp.dot(act, w_out, preferred_element_type=jnp.float32)
        side = lax.optimization_barrier(jnp.sum(slot_out * gs_rows.astype(jnp.float32), axis=1))
        dx_pad = jnp.concatenate([slot_dx, jnp.zeros((1, D), jnp.float32)], axis=0)
        side_pad = jnp.concatenate([side, jnp.zeros((1,), jnp.float32)], axis=0)
        moe_dx = moe_dx + dx_pad[target[:, 0]] + dx_pad[target[:, 1]]
        grad_gates = grad_gates + side_pad[target]
        return ((moe_dx, grad_gates), (grad_in, grad_out))
    start = (jnp.zeros((TOKENS, D), jnp.float32), jnp.zeros((TOKENS, 2), jnp.float32))
    (moe_dx, grad_gates), (grad_wide_in, grad_wide_out) = lax.scan(per_expert, start, jnp.arange(EXPERTS, dtype=jnp.int32))
    grad_mid = (out_grad.astype(jnp.float32) + moe_dx).astype(jnp.bfloat16)
    d_heads = jnp.dot(grad_mid, attn_proj.T, preferred_element_type=jnp.float32).astype(jnp.bfloat16)
    seq_count = TOKENS // SEQ

    def per_sequence(pieces):
        return sequence_backward(pieces[0], pieces[1], pieces[2], pieces[3], pieces[4])
    shaped = (queries.reshape(seq_count, SEQ, D), key_rows.reshape(seq_count, SEQ, D), value_head_rows.reshape(seq_count, SEQ, D), d_heads.reshape(seq_count, SEQ, D), seq_lengths)
    grad_q, grad_k, grad_v, attention_mixture = lax.map(per_sequence, shaped)
    grad_q = grad_q.reshape(TOKENS, D)
    grad_k = grad_k.reshape(TOKENS, D)
    grad_v = grad_v.reshape(TOKENS, D)
    attention_mixture = attention_mixture.reshape(TOKENS, D)
    grad_proj = jnp.dot(attention_mixture.T, grad_mid, preferred_element_type=jnp.float32).astype(jnp.bfloat16)
    return (grad_mid, grad_q, grad_k, grad_v, grad_gates, grad_wide_in, grad_wide_out, grad_proj)
```

```python
import math

import jax
import jax.numpy as jnp
import numpy as np
from jax import lax
from jax.experimental import pallas as pl
from jax.experimental.pallas import tpu as pltpu
from jax.sharding import PartitionSpec as P

HEAD_SIZE = 64
GELU_C = 0.7978845608028654
GELU_A = 0.044715
MESH = pl.DeviceIdType.MESH

NZ, NQ, NP = 8, 8, 16
CAP = 5
TOK = 128
D = 1024
ROWS = 2 * NQ * CAP
ALL = NZ * ROWS
KC, CW = 4, 256
HALF = D // 2
EXT = HALF + 128
BLK = 4 * ROWS
F32 = jnp.float32
BF16 = jnp.bfloat16


def group_slots(choices, experts, capacity):
    count = choices.shape[0]
    order = jnp.concatenate([choices[:, 0], choices[:, 1]])
    onehot = (order[:, None] == jnp.arange(experts, dtype=jnp.int32)[None, :]).astype(jnp.int32)
    before = jnp.cumsum(onehot, axis=0) - onehot
    place = jnp.sum(before * onehot, axis=1)
    place = jnp.where(place < capacity, place, -1)
    return place.reshape(2, count)


def dot_nn(a, b):
    return jnp.dot(a, b, preferred_element_type=F32)


def dot_nt(a, b):
    return lax.dot_general(a, b, (((1,), (1,)), ((), ())), preferred_element_type=F32)


def dot_tn(a, b):
    return lax.dot_general(a, b, (((0,), (0,)), ((), ())), preferred_element_type=F32)


def swap_table():
    out = np.arange(ALL)
    z, rest = out // ROWS, out % ROWS
    core, rest = rest // (NQ * CAP), rest % (NQ * CAP)
    q, s = rest // CAP, rest % CAP
    table = np.zeros((ALL, ALL), np.float32)
    table[out, q * ROWS + core * NQ * CAP + z * CAP + s] = 1.0
    return table


def moe_kernel(
    rowidx, gate, x_ref, g_ref, mixt, swap, w_in_hbm, w_out_hbm,
    mid, gates, grad_in, grad_out, proj,
    w_in, w_out, m_buf, m_send, t_buf, t_use, sa, ra, sb, rr,
    pre, dact, act, dpre, side, ds, dr, do, sbr, rbr, yy, sar, rar, fs, fr,
    rs_s, rs_r, rs_o, rs_b, rs2, rs_c, rs3,
    w_sem, m_ss, m_rs, t_ss, t_rs, a_ss, a_rs, b_ss, b_rs, c_ss, c_rs,
    cr_ss, cr_rs, br_ss, br_rs, ar_ss, ar_rs, f_ss, f_rs, p1_ss, p1_rs, p2_ss, p2_rs, p3_ss, p3_rs,
):
    e = lax.axis_index("expert")
    r = lax.axis_index("replica")
    z, q, xh, c = e // NQ, e % NQ, r // 2, r % 2
    pm = xh * NQ + q
    other = 1 - c
    partner = (e, xh * 2 + other)

    def dev_z(j):
        return (((z + j) % NZ) * NQ + q, r)

    def plane_of(j):
        return (pm + j) % NP

    def dev_p(j):
        p = plane_of(j)
        return (z * NQ + p % NQ, (p // NQ) * 2 + c)

    def remote(src, dst, ss, rs, dev):
        return pltpu.make_async_remote_copy(
            src_ref=src, dst_ref=dst, send_sem=ss, recv_sem=rs, device_id=dev, device_id_type=MESH
        )

    load_in = pltpu.make_async_copy(w_in_hbm, w_in, w_sem.at[0])
    load_out = pltpu.make_async_copy(w_out_hbm, w_out, w_sem.at[1])
    load_in.start()
    load_out.start()

    bar = pltpu.get_barrier_semaphore()

    def greet_z(j, _):
        pl.semaphore_signal(bar, inc=1, device_id=dev_z(j), device_id_type=MESH)
        return 0

    def greet_p(j, _):
        pl.semaphore_signal(bar, inc=1, device_id=dev_p(j), device_id_type=MESH)
        return 0

    pl.semaphore_signal(bar, inc=1, device_id=partner, device_id_type=MESH)
    lax.fori_loop(1, NZ, greet_z, 0)
    lax.fori_loop(1, NP, greet_p, 0)

    rows_of = lax.broadcasted_iota(jnp.int32, (ALL, TOK), 0)
    signed = jnp.where(rows_of == rowidx[0:1, :], gate[0:1, :], 0.0) - jnp.where(
        rows_of == rowidx[1:2, :], gate[1:2, :], 0.0
    )
    t_buf[c] = signed.astype(BF16)

    @pl.when(c == 0)
    def _():
        m_buf[0] = x_ref[...]
        m_send[...] = g_ref[...]

    @pl.when(c == 1)
    def _():
        m_buf[1] = g_ref[...]
        m_send[...] = x_ref[...]

    pl.semaphore_wait(bar, NZ + NP - 1)

    m_copy = remote(m_send, m_buf.at[c], m_ss, m_rs, partner)
    t_copy = remote(t_buf.at[c], t_buf.at[c], t_ss, t_rs, partner)
    t_copy.start()
    m_copy.start()
    t_copy.wait_recv()
    for j in range(2):
        size = jnp.abs(t_buf[j].astype(F32))
        t_use[j] = jnp.where(c == 0, jnp.where(size > 0.0, 1.0, 0.0), size).astype(BF16)
    m_copy.wait_recv()

    def copy_a(k, j):
        return remote(sa.at[k, j], ra.at[k, (NZ - j) % NZ], a_ss.at[k, j], a_rs.at[k, (NZ - j) % NZ], dev_z(j))

    def recv_a(k, j):
        return remote(sa.at[k, j], ra.at[k, j], a_ss.at[k, j], a_rs.at[k, j], dev_z(j))

    def copy_b(k, j):
        return remote(
            sb.at[k, plane_of(j) % NQ], rr.at[c, k, (NP - j) % NP], b_ss.at[k, j], b_rs.at[k, (NP - j) % NP], dev_p(j)
        )

    def recv_b(k, j):
        return remote(sb.at[k, 0], rr.at[c, k, j], b_ss.at[k, j], b_rs.at[k, j], dev_p(j))

    def copy_c(k):
        return remote(rr.at[c, k], rr.at[c, k], c_ss.at[k], c_rs.at[k], partner)

    def recv_c(k):
        return remote(rr.at[other, k], rr.at[other, k], c_ss.at[k], c_rs.at[k], partner)

    def each(count, body):
        def step(j, _):
            body(j)
            return 0

        lax.fori_loop(1, count, step, 0)

    for k in range(KC):
        cols = slice(k * CW, (k + 1) * CW)
        rows = dot_nn(t_use[0], m_buf[0, :, cols]) + dot_nn(t_use[1], m_buf[1, :, cols])
        sa[k] = rows.astype(BF16).reshape(NZ, ROWS, CW)
        each(NZ, lambda j: copy_a(k, j).start())
        ra[k, 0] = sa[k, 0]

    def stage_b(k):
        each(NZ, lambda j: recv_a(k, j).wait_recv())
        rows = dot_nn(swap[...], ra[k].reshape(ALL, CW))
        sb[k] = rows.astype(BF16).reshape(NQ, ROWS, CW)
        each(NP, lambda j: copy_b(k, j).start())
        rr[c, k, 0] = sb[k, q]

    def stage_c(k):
        each(NP, lambda j: recv_b(k, j).wait_recv())
        copy_c(k).start()

    def stage_d(k):
        recv_c(k).wait_recv()
        if k == 0:
            load_in.wait()
            load_out.wait()

        def body(i, _):
            xk = rr[0, k, pl.ds(4 * i, 4)].reshape(BLK, CW)
            gk = rr[1, k, pl.ds(4 * i, 4)].reshape(BLK, CW)
            p_new = dot_nn(xk, w_in[k * CW : (k + 1) * CW, :])
            d_new = dot_nt(gk, w_out[:, k * CW : (k + 1) * CW])
            if k == 0:
                pre[i] = p_new
                dact[i] = d_new
            else:
                pre[i] += p_new
                dact[i] += d_new
            return 0

        lax.fori_loop(0, 4, body, 0)

    for step in range(KC + 2):
        if step < KC:
            stage_b(step)
        if 0 <= step - 1 < KC:
            stage_c(step - 1)
        if 0 <= step - 2 < KC:
            stage_d(step - 2)

    SUB = 32
    lanes = lax.broadcasted_iota(jnp.int32, (SUB, 128), 1)

    def gelu_block(i):
        def body(n, _):
            at = pl.multiple_of(n * SUB, SUB)
            u = pre[i, pl.ds(at, SUB), :]
            da = dact[i, pl.ds(at, SUB), :]
            uu = u * u
            inner = jnp.tanh(GELU_C * (u + GELU_A * uu * u))
            half = 0.5 * (1.0 + inner)
            a = (u * half).astype(BF16)
            slope = half + 0.5 * u * (1.0 - inner * inner) * (GELU_C + (3.0 * GELU_A * GELU_C) * uu)
            dp = (da * slope).astype(BF16)
            s = jnp.sum(a.astype(F32) * da, axis=1, keepdims=True)
            hi = s.astype(BF16).astype(F32)
            to = pl.multiple_of(i * BLK + at, SUB)
            side[pl.ds(to, SUB), :] = jnp.where(lanes == 0, hi, jnp.where(lanes == 1, s - hi, 0.0)).astype(BF16)
            for f in range(KC):
                act[f, pl.ds(to, SUB), :] = a[:, f * CW : (f + 1) * CW]
                dpre[f, pl.ds(to, SUB), :] = dp[:, f * CW : (f + 1) * CW]
            return 0

        lax.fori_loop(0, BLK // SUB, body, 0)

    def dx_block(i):
        rows = pl.ds(i * BLK, BLK)

        def half_of(h):
            total = None
            for f in range(KC):
                term = dot_nt(
                    dpre[f, rows, :], w_in[pl.ds(pl.multiple_of(h * HALF, HALF), HALF), f * CW : (f + 1) * CW]
                )
                total = term if total is None else total + term
            return total

        ds[i] = half_of(other).astype(BF16).reshape(4, ROWS, HALF)
        copy_cr(i).start()
        do[i] = half_of(c)

    def copy_cr(i):
        return remote(ds.at[i], dr.at[i], cr_ss.at[i], cr_rs.at[i], partner)

    def copy_br(j):
        return remote(sbr.at[j], rbr.at[(NP - j) % NP], br_ss.at[j], br_rs.at[(NP - j) % NP], dev_p(j))

    def recv_br(j):
        return remote(sbr.at[j], rbr.at[j], br_ss.at[j], br_rs.at[j], dev_p(j))

    def return_block(i):
        copy_cr(i).wait_recv()
        for n in range(4):
            rows = slice(n * ROWS, (n + 1) * ROWS)
            sbr[4 * i + n, :, 0:HALF] = (do[i, rows, :] + dr[i, n].astype(F32)).astype(BF16)
            sbr[4 * i + n, :, HALF:EXT] = side[i * BLK + n * ROWS : i * BLK + (n + 1) * ROWS, :]
            if 4 * i + n:
                copy_br(4 * i + n).start()

    for i in range(5):
        if i < 4:
            gelu_block(i)
            dx_block(i)
        if i > 0:
            return_block(i - 1)

    def wide_in_body(n, _):
        at = pl.multiple_of((n // KC) * CW, CW)
        f = n % KC
        rows = rr[0, n // KC].reshape(NP * ROWS, CW)
        term = dot_tn(rows, dpre[f]).astype(BF16)
        grad_in[pl.ds(at, CW), pl.ds(pl.multiple_of(f * CW, CW), CW)] = term
        return 0

    def wide_out_body(n, _):
        f = n // KC
        k = n % KC
        rows = rr[1, k].reshape(NP * ROWS, CW)
        term = dot_tn(act[f], rows).astype(BF16)
        grad_out[pl.ds(pl.multiple_of(f * CW, CW), CW), pl.ds(pl.multiple_of(k * CW, CW), CW)] = term
        return 0

    lax.fori_loop(0, KC * KC, wide_in_body, 0)

    each(NP, lambda j: recv_br(j).wait_recv())
    lanes_r = lax.broadcasted_iota(jnp.int32, (ROWS, 128), 1)
    for j in range(NQ):
        one = sbr if j == 0 else rbr
        to = (q + j) % NQ
        yy[to, :, 0:HALF] = (one[j, :, 0:HALF].astype(F32) + rbr[j + NQ, :, 0:HALF].astype(F32)).astype(BF16)
        s = jnp.sum(
            one[j, :, HALF:EXT].astype(F32) + rbr[j + NQ, :, HALF:EXT].astype(F32), axis=1, keepdims=True
        )
        hi = s.astype(BF16).astype(F32)
        yy[to, :, HALF:EXT] = jnp.where(lanes_r == 0, hi, jnp.where(lanes_r == 1, s - hi, 0.0)).astype(BF16)
    sar[...] = dot_nn(swap[...], yy[...].reshape(ALL, EXT)).astype(BF16).reshape(NZ, ROWS, EXT)

    def copy_ar(j):
        return remote(sar.at[j], rar.at[(NZ - j) % NZ], ar_ss.at[j], ar_rs.at[(NZ - j) % NZ], dev_z(j))

    def recv_ar(j):
        return remote(sar.at[j], rar.at[j], ar_ss.at[j], ar_rs.at[j], dev_z(j))

    each(NZ, lambda j: copy_ar(j).start())
    rar[0] = sar[0]
    lax.fori_loop(0, KC * KC, wide_out_body, 0)
    each(NZ, lambda j: recv_ar(j).wait_recv())

    def home(j):
        t = t_buf[j].astype(F32)
        any_t = jnp.where(t != 0.0, 1.0, 0.0).astype(BF16)
        first = jnp.where(t > 0.0, 1.0, 0.0).astype(BF16)
        second = jnp.where(t < 0.0, 1.0, 0.0).astype(BF16)
        rows = rar[...].reshape(ALL, EXT)
        return (
            dot_tn(any_t, rows[:, 0:HALF]),
            dot_tn(first, rows[:, HALF:EXT]),
            dot_tn(second, rows[:, HALF:EXT]),
        )

    theirs = home(other)
    fs[:, 0:HALF] = theirs[0]
    fs[:, HALF : HALF + 128] = theirs[1]
    fs[:, HALF + 128 : HALF + 256] = theirs[2]
    f_copy = remote(fs, fr, f_ss, f_rs, partner)
    f_copy.start()
    ours = home(c)
    f_copy.wait_recv()
    mine_at = pl.ds(pl.multiple_of(c * HALF, HALF), HALF)
    other_at = pl.ds(pl.multiple_of(other * HALF, HALF), HALF)
    mid[:, mine_at] = (g_ref[:, mine_at].astype(F32) + ours[0]).astype(BF16)
    mid[:, other_at] = (g_ref[:, other_at].astype(F32) + fr[:, 0:HALF]).astype(BF16)
    gates[0] = ours[1] + fr[:, HALF : HALF + 128]
    gates[1] = ours[2] + fr[:, HALF + 128 : HALF + 256]

    def proj_cols(b, core):
        cols = pl.ds(pl.multiple_of(b * 512 + core * 256, 256), 256)
        return dot_nn(mixt[...], mid[:, cols])

    for b in range(2):
        rs_s[b] = proj_cols(b, other).astype(BF16).reshape(NZ, NQ, 16, 256)
    p1 = remote(rs_s, rs_r, p1_ss, p1_rs, partner)
    p1.start()
    for b in range(2):
        rs_o[b] = proj_cols(b, c).reshape(NZ, NQ, 16, 256)
    p1.wait_recv()
    for b in range(2):
        rs_b[b] = (rs_o[b] + rs_r[b].astype(F32)).astype(BF16)

    def copy_p2(j):
        p = plane_of(j)
        return remote(
            rs_b.at[p // NQ, :, p % NQ], rs2.at[(NP - j) % NP], p2_ss.at[j], p2_rs.at[(NP - j) % NP], dev_p(j)
        )

    def recv_p2(j):
        return remote(rs_b.at[0, :, 0], rs2.at[j], p2_ss.at[j], p2_rs.at[j], dev_p(j))

    each(NP, lambda j: copy_p2(j).start())
    rs2[0] = rs_b[xh, :, q]
    each(NP, lambda j: recv_p2(j).wait_recv())

    def add_p2(j, total):
        return total + rs2[j].astype(F32)

    rs_c[...] = lax.fori_loop(1, NP, add_p2, rs2[0].astype(F32)).astype(BF16)

    def copy_p3(j):
        return remote(
            rs_c.at[(z + j) % NZ], rs3.at[(NZ - j) % NZ], p3_ss.at[j], p3_rs.at[(NZ - j) % NZ], dev_z(j)
        )

    def recv_p3(j):
        return remote(rs_c.at[0], rs3.at[j], p3_ss.at[j], p3_rs.at[j], dev_z(j))

    each(NZ, lambda j: copy_p3(j).start())
    rs3[0] = rs_c[z]
    each(NZ, lambda j: recv_p3(j).wait_recv())
    proj[...] = jnp.sum(rs3[...].astype(F32), axis=0).astype(BF16)

    m_copy.wait_send()
    t_copy.wait_send()
    f_copy.wait_send()
    p1.wait_send()
    for k in range(KC):
        each(NZ, lambda j: recv_a(k, j).wait_send())
        each(NP, lambda j: recv_b(k, j).wait_send())
        copy_c(k).wait_send()
        copy_cr(k).wait_send()
    each(NP, lambda j: recv_br(j).wait_send())
    each(NZ, lambda j: recv_ar(j).wait_send())
    each(NP, lambda j: recv_p2(j).wait_send())
    each(NZ, lambda j: recv_p3(j).wait_send())


def moe(rowidx, gate, x, g, mixt, swap, w_in, w_out):
    vmem = pl.BlockSpec(memory_space=pltpu.VMEM)
    hbm = pl.BlockSpec(memory_space=pl.ANY)
    dma = pltpu.SemaphoreType.DMA
    V = pltpu.VMEM
    return pl.pallas_call(
        moe_kernel,
        out_shape=(
            jax.ShapeDtypeStruct((TOK, D), BF16),
            jax.ShapeDtypeStruct((2, TOK, 128), F32),
            jax.ShapeDtypeStruct((D, D), BF16),
            jax.ShapeDtypeStruct((D, D), BF16),
            jax.ShapeDtypeStruct((16, 256), BF16),
        ),
        in_specs=[vmem] * 6 + [hbm] * 2,
        out_specs=(vmem,) * 5,
        scratch_shapes=[
            V((D, D), BF16), V((D, D), BF16),
            V((2, TOK, D), BF16), V((TOK, D), BF16),
            V((2, ALL, TOK), BF16), V((2, ALL, TOK), BF16),
            V((KC, NZ, ROWS, CW), BF16), V((KC, NZ, ROWS, CW), BF16), V((KC, NQ, ROWS, CW), BF16),
            V((2, KC, NP, ROWS, CW), BF16),
            V((4, BLK, D), F32), V((4, BLK, D), F32),
            V((KC, NP * ROWS, CW), BF16), V((KC, NP * ROWS, CW), BF16), V((NP * ROWS, 128), BF16),
            V((4, 4, ROWS, HALF), BF16), V((4, 4, ROWS, HALF), BF16), V((4, BLK, HALF), F32),
            V((NP, ROWS, EXT), BF16), V((NP, ROWS, EXT), BF16),
            V((NQ, ROWS, EXT), BF16), V((NZ, ROWS, EXT), BF16), V((NZ, ROWS, EXT), BF16),
            V((TOK, HALF + 256), F32), V((TOK, HALF + 256), F32),
            V((2, NZ, NQ, 16, 256), BF16), V((2, NZ, NQ, 16, 256), BF16), V((2, NZ, NQ, 16, 256), F32),
            V((2, NZ, NQ, 16, 256), BF16), V((NP, NZ, 16, 256), BF16),
            V((NZ, 16, 256), BF16), V((NZ, 16, 256), BF16),
            dma((2,)), dma, dma, dma, dma,
            dma((KC, NZ)), dma((KC, NZ)), dma((KC, NP)), dma((KC, NP)), dma((KC,)), dma((KC,)),
            dma((4,)), dma((4,)), dma((NP,)), dma((NP,)), dma((NZ,)), dma((NZ,)), dma, dma, dma, dma,
            dma((NP,)), dma((NP,)), dma((NZ,)), dma((NZ,)),
        ],
        compiler_params=pltpu.CompilerParams(
            collective_id=0, has_side_effects=True, vmem_limit_bytes=62 * 1024 * 1024
        ),
        cost_estimate=pl.CostEstimate(flops=14_000_000_000, bytes_accessed=12_000_000, transcendentals=1_310_720),
    )(rowidx, gate, x, g, mixt, swap, w_in, w_out)


def attention_forward(queries, key_rows, value_head_rows, length):
    heads = queries.shape[1] // HEAD_SIZE
    scale = 1.0 / math.sqrt(HEAD_SIZE)
    spec = (queries.shape[0], heads, HEAD_SIZE)
    scores = jnp.einsum(
        "fcy,wcy->cfw", queries.reshape(spec), key_rows.reshape(spec), preferred_element_type=F32
    ) * scale
    live = jnp.arange(queries.shape[0], dtype=jnp.int32) < length
    scores = jnp.where(live[None, None, :], scores, -1000000000.0)
    top = jnp.max(scores, axis=-1, keepdims=True)
    expo = jnp.exp(scores - top)
    probs = expo / jnp.sum(expo, axis=-1, keepdims=True)
    mixt = jnp.einsum(
        "fwn,nfy->fyw", probs.astype(BF16), value_head_rows.reshape(spec), preferred_element_type=F32
    ).astype(BF16)
    return probs, mixt.reshape(queries.shape[1], queries.shape[0])


def attention_backward(queries, key_rows, value_head_rows, d_heads, probs):
    heads = queries.shape[1] // HEAD_SIZE
    scale = 1.0 / math.sqrt(HEAD_SIZE)
    spec = (queries.shape[0], heads, HEAD_SIZE)
    qmat, kmat, vmat, gmat = (a.reshape(spec) for a in (queries, key_rows, value_head_rows, d_heads))
    d_probs = jnp.einsum("fcy,wcy->cfw", gmat, vmat, preferred_element_type=F32)
    grad_v = jnp.einsum("hqk,qhd->khd", probs.astype(BF16), gmat, preferred_element_type=F32).astype(BF16)
    inner = jnp.sum(d_probs * probs, axis=-1, keepdims=True)
    dscore = (probs * (d_probs - inner)).astype(BF16)
    grad_q = (jnp.einsum("fwn,nfy->wfy", dscore, kmat, preferred_element_type=F32) * scale).astype(BF16)
    grad_k = (jnp.einsum("hqk,qhd->khd", dscore, qmat, preferred_element_type=F32) * scale).astype(BF16)
    return grad_q.reshape(queries.shape), grad_k.reshape(queries.shape), grad_v.reshape(queries.shape)


def on_device(
    mid_acts, out_grad, queries, key_rows, value_head_rows, seq_lengths,
    expert_ids, gate_probs, wide_in, wide_out, attn_proj,
):
    experts = lax.axis_size("expert")
    slots = group_slots(expert_ids, experts, CAP)
    ids = expert_ids.T
    z = lax.axis_index("expert") // NQ
    core = lax.axis_index("replica") % 2
    place = ((ids // NQ + NZ - z) % NZ) * ROWS + core * (NQ * CAP) + (ids % NQ) * CAP + slots
    rowidx = jnp.where(slots >= 0, place, -1).astype(jnp.int32)
    gate_t = gate_probs.T.astype(F32)
    probs, mixt = attention_forward(queries, key_rows, value_head_rows, seq_lengths[0])
    grad_mid, gates, grad_in, grad_out, proj = moe(
        rowidx, gate_t, mid_acts, out_grad, mixt, jnp.asarray(swap_table(), BF16), wide_in[0], wide_out[0]
    )
    grad_gates = (jnp.sum(gates, axis=2) / gate_t).T
    d_heads = dot_nt(grad_mid, attn_proj).astype(BF16)
    grad_q, grad_k, grad_v = attention_backward(queries, key_rows, value_head_rows, d_heads, probs)
    return (grad_mid, grad_q, grad_k, grad_v, grad_gates, grad_in[None], grad_out[None], proj)


def solution(mesh):
    both = ("expert", "replica")
    return jax.shard_map(
        on_device,
        mesh=mesh,
        in_specs=(
            P(both, None), P(both, None), P(both, None), P(both, None), P(both, None), P(both),
            P(both, None), P(both, None), P("expert", None, "replica"), P("expert", "replica", None), P(),
        ),
        out_specs=(
            P(both, None), P(both, None), P(both, None), P(both, None), P(both, None),
            P("expert", None, "replica"), P("expert", "replica", None), P("expert", "replica"),
        ),
        check_vma=False,
    )
```

```python
import math

import jax
import jax.numpy as jnp
from jax import lax
from jax.experimental import pallas as pl
from jax.experimental.pallas import tpu as pltpu
from jax.sharding import PartitionSpec as P

HEAD_SIZE = 64
GELU_C = 0.7978845608028654
GELU_A = 0.044715
MESH = pl.DeviceIdType.MESH

NZ, NQ, NP = 8, 8, 16
CAP = 5
TOK = 128
D = 1024
ROWS = 2 * NQ * CAP
ALL = NZ * ROWS
KC, CW = 4, 256
BLK = 4 * ROWS
F32 = jnp.float32
BF16 = jnp.bfloat16


def dot_nn(a, b):
    return jnp.dot(a, b, preferred_element_type=F32)


def dot_nt(a, b):
    return lax.dot_general(a, b, (((1,), (1,)), ((), ())), preferred_element_type=F32)


def dot_tn(a, b):
    return lax.dot_general(a, b, (((0,), (0,)), ((), ())), preferred_element_type=F32)


def moe_kernel(
    length, ids_ref, gate_ref, x_hbm, g_hbm, q_hbm, k_hbm, v_hbm, ap_hbm, w_in_hbm, w_out_hbm,
    mid, grad_q, grad_k, grad_v, gates, gin_hbm, gout_hbm, proj,
    q_buf, k_buf, v_buf, ap, probs, d_heads,
    w_in, w_arr, w_out, swap, mixt, grad_in, grad_out, xg, t_buf, t_use, t_all, t_one, sa, ra, sb, rr,
    pre, dact, act, dpre, side, ds, dr, do, sbr, rbr, yy, sar, rar,
    sp, sp_in, ys, sz, sz_in, ga, ga_in, mo, mo_in, rs_b, rs2, rs_c, rs3,
    w_sem, n_sem, o_sem, pair_ss, pair_rs, a_ss, a_rs, b_ss, b_rs, c_ss, c_rs, cr_ss, cr_rs,
    br_ss, br_rs, ar_ss, ar_rs, sp_ss, sp_rs, sz_ss, sz_rs, p2_ss, p2_rs, p3_ss, p3_rs,
):
    e = lax.axis_index("expert")
    r = lax.axis_index("replica")
    z, q, xh, c = e // NQ, e % NQ, r // 2, r % 2
    pm = xh * NQ + q
    other = 1 - c
    partner = (e, xh * 2 + other)
    late = []

    def dev_z(j):
        return (((z + j) % NZ) * NQ + q, r)

    def plane_of(j):
        return (pm + j) % NP

    def dev_p(j):
        p = plane_of(j)
        return (z * NQ + p % NQ, (p // NQ) * 2 + c)

    def remote(src, dst, ss, rs, dev):
        return pltpu.make_async_remote_copy(
            src_ref=src, dst_ref=dst, send_sem=ss, recv_sem=rs, device_id=dev, device_id_type=MESH
        )

    def pair(n, src, dst):
        return remote(src, dst, pair_ss.at[n], pair_rs.at[n], partner)

    def each(count, body):
        def step(j, _):
            body(j)
            return 0

        lax.fori_loop(1, count, step, 0)

    def piece(xhi, core, h):
        return pl.ds(pl.multiple_of(xhi * 512 + core * 256 + h * 128, 128), 128)

    tokens = [
        pltpu.make_async_copy(x_hbm, xg.at[0, c], w_sem.at[3]),
        pltpu.make_async_copy(g_hbm, xg.at[1, c], w_sem.at[4]),
    ]
    heads_in = [
        pltpu.make_async_copy(q_hbm, q_buf, w_sem.at[5]),
        pltpu.make_async_copy(k_hbm, k_buf, w_sem.at[6]),
        pltpu.make_async_copy(v_hbm, v_buf, w_sem.at[7]),
    ]
    loads = [
        pltpu.make_async_copy(w_in_hbm, w_in, w_sem.at[1]),
        pltpu.make_async_copy(w_out_hbm, w_out, w_sem.at[2]),
        pltpu.make_async_copy(ap_hbm, ap, w_sem.at[0]),
    ]
    arranged = []
    for n in range(8):
        core, h, xhi = n // 4, (n // 2) % 2, n % 2
        arranged.append(
            pltpu.make_async_copy(
                w_in_hbm.at[pl.ds(xhi * 512 + core * 256 + h * 128, 128)],
                w_arr.at[core, h, pl.ds(xhi * 128, 128)],
                n_sem.at[n],
            )
        )
    for copy in tokens + heads_in + loads + arranged:
        copy.start()

    bar = pltpu.get_barrier_semaphore()
    pl.semaphore_signal(bar, inc=1, device_id=partner, device_id_type=MESH)
    each(NZ, lambda j: pl.semaphore_signal(bar, inc=1, device_id=dev_z(j), device_id_type=MESH))
    each(NP, lambda j: pl.semaphore_signal(bar, inc=1, device_id=dev_p(j), device_id_type=MESH))

    above = lax.broadcasted_iota(jnp.int32, (TOK, TOK), 0)
    along = lax.broadcasted_iota(jnp.int32, (TOK, TOK), 1)

    def to_column(row):
        return jnp.sum(jnp.where(above == along, jnp.broadcast_to(row, (TOK, TOK)), 0), axis=1, keepdims=True)

    def count(which):
        return jnp.sum(jnp.where(which, 1, 0), axis=0, keepdims=True)

    ids = [ids_ref[k : k + 1, :] for k in range(2)]
    columns = [to_column(row) for row in ids]
    gate = [gate_ref[k : k + 1, :].astype(F32) for k in range(2)]
    slot = [
        count((columns[0] == ids[0]) & (above < along)),
        count(columns[0] == ids[1]) + count((columns[1] == ids[1]) & (above < along)),
    ]
    rows_of = lax.broadcasted_iota(jnp.int32, (ALL, TOK), 0)
    signed = None
    for k in range(2):
        place = ((ids[k] // NQ + NZ - z) % NZ) * ROWS + c * (NQ * CAP) + (ids[k] % NQ) * CAP + slot[k]
        place = jnp.where(slot[k] < CAP, place, -1)
        term = jnp.where(rows_of == place, gate[k] if k == 0 else -gate[k], 0.0)
        signed = term if signed is None else signed + term
    t_buf[c] = signed.astype(BF16)
    for copy in tokens:
        copy.wait()
    pl.semaphore_wait(bar, NZ + NP - 1)

    t_copy = pair(0, t_buf.at[c], t_buf.at[c])
    m_copy = pair(1, xg.at[other, c], xg.at[other, c])
    n_copy = pair(2, xg.at[c, c], xg.at[c, c])
    t_copy.start()
    m_copy.start()
    n_copy.start()
    late.extend([t_copy.wait_send, m_copy.wait_send, n_copy.wait_send])
    t_copy.wait_recv()
    for j in range(2):
        size = jnp.abs(t_buf[j].astype(F32))
        t_use[j] = jnp.where(c == 0, jnp.where(size > 0.0, 1.0, 0.0), size).astype(BF16)
    pair(1, xg.at[c, other], xg.at[c, other]).wait_recv()

    def copy_a(k, j):
        return remote(sa.at[k, j], ra.at[k, (NZ - j) % NZ], a_ss.at[k, j], a_rs.at[k, (NZ - j) % NZ], dev_z(j))

    def recv_a(k, j):
        return remote(sa.at[k, j], ra.at[k, j], a_ss.at[k, j], a_rs.at[k, j], dev_z(j))

    def copy_b(k, j):
        return remote(
            sb.at[k, plane_of(j) % NQ], rr.at[c, k, (NP - j) % NP], b_ss.at[k, j], b_rs.at[k, (NP - j) % NP], dev_p(j)
        )

    def recv_b(k, j):
        return remote(sb.at[k, 0], rr.at[c, k, j], b_ss.at[k, j], b_rs.at[k, j], dev_p(j))

    def copy_c(k):
        return remote(rr.at[c, k], rr.at[c, k], c_ss.at[k], c_rs.at[k], partner)

    def recv_c(k):
        return remote(rr.at[other, k], rr.at[other, k], c_ss.at[k], c_rs.at[k], partner)

    def stage_a(k):
        each(NZ, lambda j: copy_a(k, j).start())
        ra[k, 0] = sa[k, 0]

    AHEAD = 2
    for k in range(KC):
        cols = slice(k * CW, (k + 1) * CW)
        rows = dot_nn(t_use[0], xg[c, 0, :, cols]) + dot_nn(t_use[1], xg[c, 1, :, cols])
        sa[k] = rows.astype(BF16).reshape(NZ, ROWS, CW)
        if k < AHEAD:
            stage_a(k)
    left_lane = lax.broadcasted_iota(jnp.int32, (TOK, 128), 1) < HEAD_SIZE
    live = lax.broadcasted_iota(jnp.int32, (TOK, TOK), 1) < length[0]
    SCALE = 1.0 / math.sqrt(HEAD_SIZE)

    def masked(block, n):
        block = block.astype(F32)
        return (jnp.where(left_lane, block, 0.0) if n == 0 else jnp.where(left_lane, 0.0, block)).astype(BF16)

    def forward(p, _):
        at = pl.ds(pl.multiple_of(p * 128, 128), 128)
        qp, kp, vp = q_buf[:, at], k_buf[:, at], v_buf[:, at]
        out = []
        for n in range(2):
            scores = jnp.where(live, dot_nt(masked(qp, n), kp) * SCALE, -1000000000.0)
            expo = jnp.exp(scores - jnp.max(scores, axis=1, keepdims=True))
            prob = expo / jnp.sum(expo, axis=1, keepdims=True)
            probs[2 * p + n] = prob
            out.append(dot_nn(prob.astype(BF16), vp))
        mixt[c, at, :] = jnp.where(left_lane, out[0], out[1]).T.astype(BF16)
        return 0

    for copy in heads_in:
        copy.wait()
    lax.fori_loop(0, 8, forward, 0)

    row = lax.broadcasted_iota(jnp.int32, (8, ALL), 1)
    place = (row % (NQ * CAP)) // CAP * ROWS + (row % ROWS) // (NQ * CAP) * (NQ * CAP) + row // ROWS * CAP + row % CAP
    for n in range(8):
        rows = lax.broadcasted_iota(jnp.int32, (ROWS, ALL), 0) + n * ROWS
        swap[n * ROWS : (n + 1) * ROWS, :] = jnp.where(rows == place[0:1, :], 1.0, 0.0).astype(BF16)
    x_copy = pair(3, mixt.at[c], mixt.at[c])
    x_copy.start()
    late.append(x_copy.wait_send)

    def stage_b(k):
        each(NZ, lambda j: recv_a(k, j).wait_recv())
        if k + AHEAD < KC:
            stage_a(k + AHEAD)
        rows = dot_nn(swap[...], ra[k].reshape(ALL, CW))
        sb[k] = rows.astype(BF16).reshape(NQ, ROWS, CW)
        each(NP, lambda j: copy_b(k, j).start())
        rr[c, k, 0] = sb[k, q]

    def stage_c(k):
        each(NP, lambda j: recv_b(k, j).wait_recv())
        copy_c(k).start()

    def stage_d(k):
        recv_c(k).wait_recv()
        if k == 0:
            loads[0].wait()
            loads[1].wait()

        def body(i, _):
            xk = rr[0, k, pl.ds(4 * i, 4)].reshape(BLK, CW)
            gk = rr[1, k, pl.ds(4 * i, 4)].reshape(BLK, CW)
            p_new = dot_nn(xk, w_in[k * CW : (k + 1) * CW, :])
            d_new = dot_nt(gk, w_out[:, k * CW : (k + 1) * CW])
            if k == 0:
                pre[i] = p_new
                dact[i] = d_new
            else:
                pre[i] += p_new
                dact[i] += d_new
            return 0

        lax.fori_loop(0, 4, body, 0)

    for step in range(KC + 2):
        if step < KC:
            stage_b(step)
        if 0 <= step - 1 < KC:
            stage_c(step - 1)
        if 0 <= step - 2 < KC:
            stage_d(step - 2)
        if step == 1:
            loads[2].wait()
            for copy in arranged:
                copy.wait()
    for k in range(KC):
        late.append(lambda k=k: each(NZ, lambda j: recv_a(k, j).wait_send()))
        late.append(lambda k=k: each(NP, lambda j: recv_b(k, j).wait_send()))
        late.append(copy_c(k).wait_send)

    SUB = 32

    def gelu_block(i):
        def body(n, _):
            at = pl.multiple_of(n * SUB, SUB)
            u = pre[i, pl.ds(at, SUB), :]
            da = dact[i, pl.ds(at, SUB), :]
            uu = u * u
            inner = jnp.tanh(GELU_C * (u + GELU_A * uu * u))
            half = 0.5 * (1.0 + inner)
            a = (u * half).astype(BF16)
            slope = half + 0.5 * u * (1.0 - inner * inner) * (GELU_C + (3.0 * GELU_A * GELU_C) * uu)
            dp = (da * slope).astype(BF16)
            s = jnp.sum(a.astype(F32) * da, axis=1, keepdims=True)
            to = pl.multiple_of(i * BLK + at, SUB)
            side[pl.ds(to, SUB), :] = jnp.broadcast_to(s, (SUB, 128))
            for f in range(KC):
                act[f, pl.ds(to, SUB), :] = a[:, f * CW : (f + 1) * CW]
                dpre[f, pl.ds(to, SUB), :] = dp[:, f * CW : (f + 1) * CW]
            return 0

        lax.fori_loop(0, BLK // SUB, body, 0)

    def copy_cr(i):
        return remote(ds.at[i], dr.at[i], cr_ss.at[i], cr_rs.at[i], partner)

    def dx_block(i):
        def part(core, h):
            total = None
            for f in range(KC):
                term = dot_nt(dpre[f, i * BLK : (i + 1) * BLK, :], w_arr[core, h, :, f * CW : (f + 1) * CW])
                total = term if total is None else total + term
            return total

        for h in range(2):
            ds[i, h] = part(other, h).astype(BF16).reshape(4, ROWS, CW)
        copy_cr(i).start()
        late.append(copy_cr(i).wait_send)
        for h in range(2):
            do[i, h] = part(c, h)

    def copy_br(h, j):
        return remote(sbr.at[h, j], rbr.at[h, (NP - j) % NP], br_ss.at[h, j], br_rs.at[h, (NP - j) % NP], dev_p(j))

    def recv_br(h, j):
        return remote(sbr.at[h, j], rbr.at[h, j], br_ss.at[h, j], br_rs.at[h, j], dev_p(j))

    def copy_sp(j):
        return remote(sp.at[j], sp_in.at[(NP - j) % NP], sp_ss.at[j], sp_rs.at[(NP - j) % NP], dev_p(j))

    def recv_sp(j):
        return remote(sp.at[j], sp_in.at[j], sp_ss.at[j], sp_rs.at[j], dev_p(j))

    diagonal = lax.broadcasted_iota(jnp.int32, (ROWS, 128), 0) == lax.broadcasted_iota(jnp.int32, (ROWS, 128), 1)

    def return_block(i, h):
        if h == 0:
            copy_cr(i).wait_recv()
        for n in range(4):
            p = 4 * i + n
            sbr[h, p] = (do[i, h, n * ROWS : (n + 1) * ROWS, :] + dr[i, h, n].astype(F32)).astype(BF16)
            if p:
                copy_br(h, p).start()

    def side_block(i):
        for n in range(4):
            p = 4 * i + n
            row = jnp.sum(jnp.where(diagonal, side[p * ROWS : (p + 1) * ROWS, :], 0.0), axis=0, keepdims=True)
            sp[p] = jnp.broadcast_to(row, (8, 128))
            if p:
                copy_sp(p).start()

    for i in range(5):
        if i < 4:
            gelu_block(i)
            dx_block(i)
        if i > 0:
            return_block(i - 1, 0)
    for i in range(4):
        return_block(i, 1)
    for i in range(4):
        side_block(i)
    for h in range(2):
        late.append(lambda h=h: each(NP, lambda j: recv_br(h, j).wait_send()))
    late.append(lambda: each(NP, lambda j: recv_sp(j).wait_send()))

    def wide_in_body(n, _):
        at = pl.multiple_of((n // KC) * CW, CW)
        f = n % KC
        rows = rr[0, n // KC].reshape(NP * ROWS, CW)
        term = dot_tn(rows, dpre[f]).astype(BF16)
        grad_in[pl.ds(at, CW), pl.ds(pl.multiple_of(f * CW, CW), CW)] = term
        return 0

    def wide_out_body(n, _):
        f = n // KC
        k = n % KC
        rows = rr[1, k].reshape(NP * ROWS, CW)
        term = dot_tn(act[f], rows).astype(BF16)
        grad_out[pl.ds(pl.multiple_of(f * CW, CW), CW), pl.ds(pl.multiple_of(k * CW, CW), CW)] = term
        return 0

    lax.fori_loop(0, KC * KC, wide_in_body, 0)
    out_in = pltpu.make_async_copy(grad_in, gin_hbm, o_sem.at[0])
    out_in.start()
    late.append(out_in.wait)

    for j in range(2):
        t = t_buf[j].astype(F32)
        t_all[j] = jnp.where(t != 0.0, 1.0, 0.0).T.astype(BF16)
        t_one[j, 0] = jnp.where(t > 0.0, 1.0, 0.0).astype(BF16)
        t_one[j, 1] = jnp.where(t < 0.0, 1.0, 0.0).astype(BF16)

    def copy_ar(h, j):
        return remote(sar.at[h, j], rar.at[h, (NZ - j) % NZ], ar_ss.at[h, j], ar_rs.at[h, (NZ - j) % NZ], dev_z(j))

    def recv_ar(h, j):
        return remote(sar.at[h, j], rar.at[h, j], ar_ss.at[h, j], ar_rs.at[h, j], dev_z(j))

    def copy_sz(j):
        return remote(sz.at[j], sz_in.at[(NZ - j) % NZ], sz_ss.at[j], sz_rs.at[(NZ - j) % NZ], dev_z(j))

    def recv_sz(j):
        return remote(sz.at[j], sz_in.at[j], sz_ss.at[j], sz_rs.at[j], dev_z(j))

    def stage_z(h):
        each(NP, lambda j: recv_br(h, j).wait_recv())
        for j in range(NQ):
            one = sbr if j == 0 else rbr
            yy[(q + j) % NQ] = (one[h, j].astype(F32) + rbr[h, j + NQ].astype(F32)).astype(BF16)
        sar[h] = dot_nn(swap[...], yy[...].reshape(ALL, CW)).astype(BF16).reshape(NZ, ROWS, CW)
        each(NZ, lambda j: copy_ar(h, j).start())
        rar[h, 0] = sar[h, 0]
        late.append(lambda: each(NZ, lambda j: recv_ar(h, j).wait_send()))

    lanes = lax.broadcasted_iota(jnp.int32, (ROWS, 128), 1)

    def side_z():
        each(NP, lambda j: recv_sp(j).wait_recv())
        for j in range(NQ):
            one = sp if j == 0 else sp_in
            row = (one[j] + sp_in[j + NQ])[0:1, :]
            s = jnp.sum(jnp.where(diagonal, jnp.broadcast_to(row, (ROWS, 128)), 0.0), axis=1, keepdims=True)
            hi = s.astype(BF16).astype(F32)
            ys[(q + j) % NQ] = jnp.where(lanes == 0, hi, jnp.where(lanes == 1, s - hi, 0.0)).astype(BF16)
        back = dot_nn(swap[...], ys[...].reshape(ALL, 128))
        for n in range(NZ):
            s = jnp.sum(back[n * ROWS : (n + 1) * ROWS, :], axis=1, keepdims=True)
            row = jnp.sum(jnp.where(diagonal, s, 0.0), axis=0, keepdims=True)
            sz[n] = jnp.broadcast_to(row, (8, 128))
        each(NZ, lambda j: copy_sz(j).start())
        sz_in[0] = sz[0]
        late.append(lambda: each(NZ, lambda j: recv_sz(j).wait_send()))

    stage_z(0)
    lax.fori_loop(0, KC * KC // 2, wide_out_body, 0)
    stage_z(1)
    side_z()
    lax.fori_loop(KC * KC // 2, KC * KC, wide_out_body, 0)
    out_out = pltpu.make_async_copy(grad_out, gout_hbm, o_sem.at[1])
    out_out.start()
    late.append(out_out.wait)
    pair(2, xg.at[other, other], xg.at[other, other]).wait_recv()
    pair(3, mixt.at[other], mixt.at[other]).wait_recv()

    def copy_p2(h, j):
        p = plane_of(j)
        return remote(
            rs_b.at[h, p // NQ, :, p % NQ], rs2.at[h, (NP - j) % NP], p2_ss.at[h, j], p2_rs.at[h, (NP - j) % NP],
            dev_p(j),
        )

    def recv_p2(h, j):
        return remote(rs_b.at[h, 0, :, 0], rs2.at[h, j], p2_ss.at[h, j], p2_rs.at[h, j], dev_p(j))

    def mo_copy(h):
        return pair(4 + h, mo.at[h], mo_in.at[h])

    def home(h):
        each(NZ, lambda j: recv_ar(h, j).wait_recv())
        rows = rar[h].reshape(ALL, CW)
        theirs = dot_nn(t_all[other], rows)
        ours = dot_nn(t_all[c], rows)
        mine = []
        for xhi in range(2):
            lane = slice(xhi * 128, (xhi + 1) * 128)
            mo[h, :, lane] = (xg[1, other, :, piece(xhi, c, h)].astype(F32) + theirs[:, lane]).astype(BF16)
            own = (xg[1, c, :, piece(xhi, c, h)].astype(F32) + ours[:, lane]).astype(BF16)
            mid[:, piece(xhi, c, h)] = own
            mine.append(own)
        mo_copy(h).start()
        late.append(mo_copy(h).wait_send)
        for xhi in range(2):
            lane = slice(xhi * 128, (xhi + 1) * 128)
            part = dot_nn(mixt[c], mine[xhi]) + dot_nn(mixt[other], mo[h, :, lane])
            rs_b[h, xhi] = part.astype(BF16).reshape(NZ, NQ, 16, 128)
        each(NP, lambda j: copy_p2(h, j).start())
        rs2[h, 0] = rs_b[h, xh, :, q]
        late.append(lambda: each(NP, lambda j: recv_p2(h, j).wait_send()))

    home(0)
    home(1)

    for h in range(2):
        mo_copy(h).wait_recv()
        for xhi in range(2):
            mid[:, piece(xhi, other, h)] = mo_in[h, :, xhi * 128 : (xhi + 1) * 128]

    for n in range(4):
        rows = slice(n * CW, (n + 1) * CW)
        d_heads[:, rows] = dot_nt(mid[...], ap[rows, :]).astype(BF16)

    def backward(p, _):
        at = pl.ds(pl.multiple_of(p * 128, 128), 128)
        qp, kp, vp, gp = q_buf[:, at], k_buf[:, at], v_buf[:, at], d_heads[:, at]
        gq, gk, gv = [], [], []
        for n in range(2):
            prob = probs[2 * p + n]
            gv.append(dot_tn(prob.astype(BF16), gp))
            d_prob = dot_nt(masked(gp, n), vp)
            inner = jnp.sum(d_prob * prob, axis=1, keepdims=True)
            d_score = (prob * (d_prob - inner)).astype(BF16)
            gq.append(dot_nn(d_score, kp))
            gk.append(dot_tn(d_score, qp))
        grad_v[:, at] = jnp.where(left_lane, gv[0], gv[1]).astype(BF16)
        grad_q[:, at] = (jnp.where(left_lane, gq[0], gq[1]) * SCALE).astype(BF16)
        grad_k[:, at] = (jnp.where(left_lane, gk[0], gk[1]) * SCALE).astype(BF16)
        return 0

    lax.fori_loop(0, 4, backward, 0)

    for h in range(2):
        each(NP, lambda j: recv_p2(h, j).wait_recv())
        total = lax.fori_loop(1, NP, lambda j, t: t + rs2[h, j].astype(F32), rs2[h, 0].astype(F32))
        rs_c[:, :, h * 128 : (h + 1) * 128] = total.astype(BF16)

    def copy_p3(j):
        return remote(
            rs_c.at[(z + j) % NZ], rs3.at[(NZ - j) % NZ], p3_ss.at[j], p3_rs.at[(NZ - j) % NZ], dev_z(j)
        )

    def recv_p3(j):
        return remote(rs_c.at[0], rs3.at[j], p3_ss.at[j], p3_rs.at[j], dev_z(j))

    each(NZ, lambda j: copy_p3(j).start())
    rs3[0] = rs_c[z]
    late.append(lambda: each(NZ, lambda j: recv_p3(j).wait_send()))

    each(NZ, lambda j: recv_sz(j).wait_recv())
    row16 = lax.broadcasted_iota(jnp.int32, (16, 128), 0)

    def gate_terms(j):
        out = []
        for k in range(2):
            total = None
            for n in range(NZ):
                row = sz_in[n][0:1, :]
                hi = row.astype(BF16).astype(F32)
                both = jnp.where(row16 == 0, hi, jnp.where(row16 == 1, row - hi, 0.0)).astype(BF16)
                term = dot_nn(both[:, 0:ROWS], t_one[j, k, n * ROWS : (n + 1) * ROWS, :])
                total = term if total is None else total + term
            out.append(jnp.sum(total, axis=0, keepdims=True))
        return jnp.concatenate(out + [jnp.zeros((6, 128), F32)], axis=0)

    ga[...] = gate_terms(other)
    ga_copy = pair(6, ga, ga_in)
    ga_copy.start()
    late.append(ga_copy.wait_send)
    ours = gate_terms(c)
    lax.fori_loop(4, 8, backward, 0)
    ga_copy.wait_recv()
    for k in range(2):
        gates[k : k + 1, :] = (ours[k : k + 1, :] + ga_in[k : k + 1, :]) / gate[k]

    each(NZ, lambda j: recv_p3(j).wait_recv())
    proj[...] = jnp.sum(rs3[...].astype(F32), axis=0).astype(BF16)

    for wait in late:
        wait()


def moe(lengths, ids, gate, x, g, q, k, v, ap, w_in, w_out):
    vmem = pl.BlockSpec(memory_space=pltpu.VMEM)
    smem = pl.BlockSpec(memory_space=pltpu.SMEM)
    hbm = pl.BlockSpec(memory_space=pl.ANY)
    V = pltpu.VMEM

    def dma(*shape):
        return [pltpu.SemaphoreType.DMA(shape)] * 2

    return pl.pallas_call(
        moe_kernel,
        out_shape=(
            *[jax.ShapeDtypeStruct((TOK, D), BF16)] * 4,
            jax.ShapeDtypeStruct((2, TOK), F32),
            jax.ShapeDtypeStruct((D, D), BF16),
            jax.ShapeDtypeStruct((D, D), BF16),
            jax.ShapeDtypeStruct((16, 256), BF16),
        ),
        in_specs=[smem, vmem, vmem] + [hbm] * 8,
        out_specs=(*[vmem] * 5, hbm, hbm, vmem),
        scratch_shapes=[
            V((TOK, D), BF16), V((TOK, D), BF16), V((TOK, D), BF16), V((D, D), BF16), V((16, TOK, TOK), F32), V((TOK, D), BF16),
            V((D, D), BF16), V((2, 2, 256, D), BF16), V((D, D), BF16), V((ALL, ALL), BF16), V((2, D, TOK), BF16),
            V((D, D), BF16), V((D, D), BF16), V((2, 2, TOK, D), BF16),
            V((2, ALL, TOK), BF16), V((2, ALL, TOK), BF16), V((2, TOK, ALL), BF16), V((2, 2, ALL, TOK), BF16),
            V((KC, NZ, ROWS, CW), BF16), V((KC, NZ, ROWS, CW), BF16), V((KC, NQ, ROWS, CW), BF16),
            V((2, KC, NP, ROWS, CW), BF16),
            V((4, BLK, D), F32), V((4, BLK, D), F32),
            V((KC, NP * ROWS, CW), BF16), V((KC, NP * ROWS, CW), BF16), V((NP * ROWS, 128), F32),
            V((4, 2, 4, ROWS, CW), BF16), V((4, 2, 4, ROWS, CW), BF16), V((4, 2, BLK, CW), F32),
            V((2, NP, ROWS, CW), BF16), V((2, NP, ROWS, CW), BF16),
            V((NQ, ROWS, CW), BF16), V((2, NZ, ROWS, CW), BF16), V((2, NZ, ROWS, CW), BF16),
            V((NP, 8, 128), F32), V((NP, 8, 128), F32), V((NQ, ROWS, 128), BF16),
            V((NZ, 8, 128), F32), V((NZ, 8, 128), F32), V((8, 128), F32), V((8, 128), F32),
            V((2, TOK, CW), BF16), V((2, TOK, CW), BF16),
            V((2, 2, NZ, NQ, 16, 128), BF16), V((2, NP, NZ, 16, 128), BF16),
            V((NZ, 16, 256), BF16), V((NZ, 16, 256), BF16),
            pltpu.SemaphoreType.DMA((8,)), pltpu.SemaphoreType.DMA((8,)), pltpu.SemaphoreType.DMA((2,)),
            *dma(7), *dma(KC, NZ), *dma(KC, NP), *dma(KC), *dma(4),
            *dma(2, NP), *dma(2, NZ), *dma(NP), *dma(NZ), *dma(2, NP), *dma(NZ),
        ],
        compiler_params=pltpu.CompilerParams(
            collective_id=0, has_side_effects=True, vmem_limit_bytes=62 * 1024 * 1024
        ),
        cost_estimate=pl.CostEstimate(flops=14_000_000_000, bytes_accessed=12_000_000, transcendentals=1_310_720),
    )(lengths, ids, gate, x, g, q, k, v, ap, w_in, w_out)


def on_device(
    mid_acts, out_grad, queries, key_rows, value_head_rows, seq_lengths,
    expert_ids, gate_probs, wide_in, wide_out, attn_proj,
):
    grad_mid, grad_q, grad_k, grad_v, grad_gates, grad_in, grad_out, proj = moe(
        seq_lengths, expert_ids.T, gate_probs.T, mid_acts, out_grad, queries, key_rows, value_head_rows, attn_proj,
        wide_in[0], wide_out[0],
    )
    return (grad_mid, grad_q, grad_k, grad_v, grad_gates.T, grad_in[None], grad_out[None], proj)


def solution(mesh):
    both = ("expert", "replica")
    return jax.shard_map(
        on_device,
        mesh=mesh,
        in_specs=(
            P(both, None), P(both, None), P(both, None), P(both, None), P(both, None), P(both),
            P(both, None), P(both, None), P("expert", None, "replica"), P("expert", "replica", None), P(),
        ),
        out_specs=(
            P(both, None), P(both, None), P(both, None), P(both, None), P(both, None),
            P("expert", None, "replica"), P("expert", "replica", None), P("expert", "replica"),
        ),
        check_vma=False,
    )
```

```python
import functools
import math

import jax
import jax.numpy as jnp
from jax import lax
from jax.experimental import pallas as pl
from jax.experimental.pallas import tpu as pltpu
from jax.sharding import PartitionSpec as P

HEAD_SIZE = 64
GELU_C = 0.7978845608028654
GELU_A = 0.044715
MESH = pl.DeviceIdType.MESH

NZ, NQ, NP = 8, 8, 16
CAP = 5
TOK = 128
D = 1024
ROWS = 2 * NQ * CAP
ALL = NZ * ROWS
KC, CW = 4, 256
BLK = 4 * ROWS
F32 = jnp.float32
BF16 = jnp.bfloat16


def dot_nn(a, b):
    return jnp.dot(a, b, preferred_element_type=F32)


def dot_nt(a, b):
    return lax.dot_general(a, b, (((1,), (1,)), ((), ())), preferred_element_type=F32)


def dot_tn(a, b):
    return lax.dot_general(a, b, (((0,), (0,)), ((), ())), preferred_element_type=F32)


def moe_kernel(
    length, ids_ref, gate_ref, x_hbm, g_hbm, q_hbm, k_hbm, v_hbm, ap_hbm, w_in_hbm, w_out_hbm,
    mid, grad_q, grad_k, grad_v, gates, gin_hbm, gout_hbm, proj,
    q_buf, k_buf, v_buf, ap, probs, d_heads,
    w_in, w_arr, w_out, swap, mixt, grad_in, grad_out, xg, t_buf, t_use, t_all, t_one, sa, ra, sb, rr,
    pre, dact, act, dpre, side, ds, dr, do, sbr, rbr, yy, sar, rar,
    sp, sp_in, ys, sz, sz_in, ga, ga_in, mo, mo_in, rs_b, rs2, rs_c, rs3,
    w_sem, n_sem, o_sem, pair_ss, pair_rs, a_ss, a_rs, b_ss, b_rs, c_ss, c_rs, cr_ss, cr_rs,
    br_ss, br_rs, ar_ss, ar_rs, sp_ss, sp_rs, sz_ss, sz_rs, p2_ss, p2_rs, p3_ss, p3_rs,
):
    e = lax.axis_index("expert")
    r = lax.axis_index("replica")
    z, q, xh, c = e // NQ, e % NQ, r // 2, r % 2
    other = 1 - c
    partner = (e, xh * 2 + other)
    late = []

    def dev_z(j):
        return (((z + j) % NZ) * NQ + q, r)

    def plane_of(j):
        i, n = j // 4, j % 4
        x = (xh * 2 + q // 4 + n) % 4
        return x // 2 * NQ + x % 2 * 4 + (q + n + i) % 4

    def back(j):
        return (4 - j // 4) % 4 * 4 + (4 - j % 4) % 4

    def twin(j):
        return (j // 4 + 2) % 4 * 4 + (j % 4 + 2) % 4

    def dev_p(j):
        p = plane_of(j)
        return (z * NQ + p % NQ, (p // NQ) * 2 + c)

    def remote(src, dst, ss, rs, dev):
        return pltpu.make_async_remote_copy(
            src_ref=src, dst_ref=dst, send_sem=ss, recv_sem=rs, device_id=dev, device_id_type=MESH
        )

    def pair(n, src, dst):
        return remote(src, dst, pair_ss.at[n], pair_rs.at[n], partner)

    def each(count, body):
        def step(j, _):
            body(j)
            return 0

        lax.fori_loop(1, count, step, 0)

    def piece(xhi, core, h):
        return pl.ds(pl.multiple_of(xhi * 512 + core * 256 + h * 128, 128), 128)

    tokens = [
        pltpu.make_async_copy(x_hbm, xg.at[0, c], w_sem.at[3]),
        pltpu.make_async_copy(g_hbm, xg.at[1, c], w_sem.at[4]),
    ]
    heads_in = [
        pltpu.make_async_copy(q_hbm, q_buf, w_sem.at[5]),
        pltpu.make_async_copy(k_hbm, k_buf, w_sem.at[6]),
        pltpu.make_async_copy(v_hbm, v_buf, w_sem.at[7]),
    ]
    loads = [
        pltpu.make_async_copy(w_in_hbm, w_in, w_sem.at[1]),
        pltpu.make_async_copy(w_out_hbm, w_out, w_sem.at[2]),
        pltpu.make_async_copy(ap_hbm, ap, w_sem.at[0]),
    ]
    arranged = []
    for n in range(8):
        core, h, xhi = n // 4, (n // 2) % 2, n % 2
        arranged.append(
            pltpu.make_async_copy(
                w_in_hbm.at[pl.ds(xhi * 512 + core * 256 + h * 128, 128)],
                w_arr.at[core, h, pl.ds(xhi * 128, 128)],
                n_sem.at[n],
            )
        )
    for copy in tokens + heads_in + loads + arranged:
        copy.start()

    bar = pltpu.get_barrier_semaphore()
    pl.semaphore_signal(bar, inc=1, device_id=partner, device_id_type=MESH)
    each(NZ, lambda j: pl.semaphore_signal(bar, inc=1, device_id=dev_z(j), device_id_type=MESH))
    each(NP, lambda j: pl.semaphore_signal(bar, inc=1, device_id=dev_p(j), device_id_type=MESH))

    above = lax.broadcasted_iota(jnp.int32, (TOK, TOK), 0)
    along = lax.broadcasted_iota(jnp.int32, (TOK, TOK), 1)

    def to_column(row):
        return jnp.sum(jnp.where(above == along, jnp.broadcast_to(row, (TOK, TOK)), 0), axis=1, keepdims=True)

    def count(which):
        return jnp.sum(jnp.where(which, 1, 0), axis=0, keepdims=True)

    ids = [ids_ref[k : k + 1, :] for k in range(2)]
    columns = [to_column(row) for row in ids]
    gate = [gate_ref[k : k + 1, :].astype(F32) for k in range(2)]
    slot = [
        count((columns[0] == ids[0]) & (above < along)),
        count(columns[0] == ids[1]) + count((columns[1] == ids[1]) & (above < along)),
    ]
    rows_of = lax.broadcasted_iota(jnp.int32, (ALL, TOK), 0)
    signed = None
    for k in range(2):
        place = ((ids[k] // NQ + NZ - z) % NZ) * ROWS + c * (NQ * CAP) + (ids[k] % NQ) * CAP + slot[k]
        place = jnp.where(slot[k] < CAP, place, -1)
        term = jnp.where(rows_of == place, gate[k] if k == 0 else -gate[k], 0.0)
        signed = term if signed is None else signed + term
    t_buf[c] = signed.astype(BF16)
    for copy in tokens:
        copy.wait()
    pl.semaphore_wait(bar, NZ + NP - 1)

    t_copy = pair(0, t_buf.at[c], t_buf.at[c])
    m_copy = pair(1, xg.at[other, c], xg.at[other, c])
    n_copy = pair(2, xg.at[c, c], xg.at[c, c])
    t_copy.start()
    m_copy.start()
    n_copy.start()
    late.extend([t_copy.wait_send, m_copy.wait_send, n_copy.wait_send])
    t_copy.wait_recv()
    for j in range(2):
        size = jnp.abs(t_buf[j].astype(F32))
        t_use[j] = jnp.where(c == 0, jnp.where(size > 0.0, 1.0, 0.0), size).astype(BF16)
    pair(1, xg.at[c, other], xg.at[c, other]).wait_recv()

    def copy_a(k, j):
        return remote(sa.at[k, j], ra.at[k, (NZ - j) % NZ], a_ss.at[k], a_rs.at[k], dev_z(j))

    def recv_a(k):
        group = ra.at[k, pl.ds(1, NZ - 1)]
        return remote(group, group, a_ss.at[k], a_rs.at[k], dev_z(1))

    def copy_b(k, j):
        return remote(
            sb.at[k, plane_of(j) % NQ], rr.at[c, k, back(j)], b_ss.at[k], b_rs.at[k], dev_p(j)
        )

    def recv_b(k):
        group = rr.at[c, k, pl.ds(1, NP - 1)]
        return remote(group, group, b_ss.at[k], b_rs.at[k], dev_p(1))

    def copy_c(k):
        return remote(rr.at[c, k], rr.at[c, k], c_ss.at[k], c_rs.at[k], partner)

    def recv_c(k):
        return remote(rr.at[other, k], rr.at[other, k], c_ss.at[k], c_rs.at[k], partner)

    def stage_a(k):
        each(NZ, lambda j: copy_a(k, j).start())
        ra[k, 0] = sa[k, 0]

    AHEAD = 2
    for k in range(KC):
        cols = slice(k * CW, (k + 1) * CW)
        rows = dot_nn(t_use[0], xg[c, 0, :, cols]) + dot_nn(t_use[1], xg[c, 1, :, cols])
        sa[k] = rows.astype(BF16).reshape(NZ, ROWS, CW)
        if k < AHEAD:
            stage_a(k)
    left_lane = lax.broadcasted_iota(jnp.int32, (TOK, 128), 1) < HEAD_SIZE
    live = lax.broadcasted_iota(jnp.int32, (TOK, TOK), 1) < length[0]
    SCALE = 1.0 / math.sqrt(HEAD_SIZE)

    def masked(block, n):
        block = block.astype(F32)
        return (jnp.where(left_lane, block, 0.0) if n == 0 else jnp.where(left_lane, 0.0, block)).astype(BF16)

    def forward(p, _):
        at = pl.ds(pl.multiple_of(p * 128, 128), 128)
        qp, kp, vp = q_buf[:, at], k_buf[:, at], v_buf[:, at]
        out = []
        for n in range(2):
            scores = jnp.where(live, dot_nt(masked(qp, n), kp) * SCALE, -1000000000.0)
            expo = jnp.exp(scores - jnp.max(scores, axis=1, keepdims=True))
            prob = expo / jnp.sum(expo, axis=1, keepdims=True)
            probs[2 * p + n] = prob
            out.append(dot_nn(prob.astype(BF16), vp))
        mixt[c, at, :] = jnp.where(left_lane, out[0], out[1]).T.astype(BF16)
        return 0

    for copy in heads_in:
        copy.wait()
    lax.fori_loop(0, 8, forward, 0)

    row = lax.broadcasted_iota(jnp.int32, (8, ALL), 1)
    place = (row % (NQ * CAP)) // CAP * ROWS + (row % ROWS) // (NQ * CAP) * (NQ * CAP) + row // ROWS * CAP + row % CAP
    for n in range(8):
        rows = lax.broadcasted_iota(jnp.int32, (ROWS, ALL), 0) + n * ROWS
        swap[n * ROWS : (n + 1) * ROWS, :] = jnp.where(rows == place[0:1, :], 1.0, 0.0).astype(BF16)
    x_copy = pair(3, mixt.at[c], mixt.at[c])
    x_copy.start()
    late.append(x_copy.wait_send)

    def stage_b(k):
        recv_a(k).wait_recv()
        if k + AHEAD < KC:
            stage_a(k + AHEAD)
        rows = dot_nn(swap[...], ra[k].reshape(ALL, CW))
        sb[k] = rows.astype(BF16).reshape(NQ, ROWS, CW)
        each(NP, lambda j: copy_b(k, j).start())
        rr[c, k, 0] = sb[k, q]

    def stage_c(k):
        recv_b(k).wait_recv()
        copy_c(k).start()

    def stage_d(k):
        recv_c(k).wait_recv()
        if k == 0:
            loads[0].wait()
            loads[1].wait()

        def body(i, _):
            xk = rr[0, k, pl.ds(4 * i, 4)].reshape(BLK, CW)
            gk = rr[1, k, pl.ds(4 * i, 4)].reshape(BLK, CW)
            p_new = dot_nn(xk, w_in[k * CW : (k + 1) * CW, :])
            d_new = dot_nt(gk, w_out[:, k * CW : (k + 1) * CW])
            if k == 0:
                pre[i] = p_new
                dact[i] = d_new
            else:
                pre[i] += p_new
                dact[i] += d_new
            return 0

        lax.fori_loop(0, 4, body, 0)

    for step in range(KC + 2):
        if step < KC:
            stage_b(step)
        if 0 <= step - 1 < KC:
            stage_c(step - 1)
        if 0 <= step - 2 < KC:
            stage_d(step - 2)
        if step == 1:
            loads[2].wait()
            for copy in arranged:
                copy.wait()
    for k in range(KC):
        late.append(lambda k=k: recv_a(k).wait_send())
        late.append(lambda k=k: recv_b(k).wait_send())
        late.append(copy_c(k).wait_send)

    SUB = 32

    def gelu_block(i):
        def body(n, _):
            at = pl.multiple_of(n * SUB, SUB)
            u = pre[i, pl.ds(at, SUB), :]
            da = dact[i, pl.ds(at, SUB), :]
            uu = u * u
            inner = jnp.tanh(GELU_C * (u + GELU_A * uu * u))
            half = 0.5 * (1.0 + inner)
            a = (u * half).astype(BF16)
            slope = half + 0.5 * u * (1.0 - inner * inner) * (GELU_C + (3.0 * GELU_A * GELU_C) * uu)
            dp = (da * slope).astype(BF16)
            s = jnp.sum(a.astype(F32) * da, axis=1, keepdims=True)
            to = pl.multiple_of(i * BLK + at, SUB)
            side[pl.ds(to, SUB), :] = jnp.broadcast_to(s, (SUB, 128))
            for f in range(KC):
                act[f, pl.ds(to, SUB), :] = a[:, f * CW : (f + 1) * CW]
                dpre[f, pl.ds(to, SUB), :] = dp[:, f * CW : (f + 1) * CW]
            return 0

        lax.fori_loop(0, BLK // SUB, body, 0)

    def copy_cr(i):
        return remote(ds.at[i], dr.at[i], cr_ss.at[i], cr_rs.at[i], partner)

    def dx_block(i):
        def part(core, h):
            total = None
            for f in range(KC):
                term = dot_nt(dpre[f, i * BLK : (i + 1) * BLK, :], w_arr[core, h, :, f * CW : (f + 1) * CW])
                total = term if total is None else total + term
            return total

        for h in range(2):
            ds[i, h] = part(other, h).astype(BF16).reshape(4, ROWS, CW)
        copy_cr(i).start()
        late.append(copy_cr(i).wait_send)
        for h in range(2):
            do[i, h] = part(c, h)

    def copy_br(h, j):
        return remote(sbr.at[h, j], rbr.at[h, back(j)], br_ss.at[h], br_rs.at[h], dev_p(j))

    def recv_br(h):
        group = rbr.at[h, pl.ds(1, NP - 1)]
        return remote(group, group, br_ss.at[h], br_rs.at[h], dev_p(1))

    def copy_sp(j):
        return remote(sp.at[j], sp_in.at[back(j)], sp_ss, sp_rs, dev_p(j))

    def recv_sp():
        group = sp_in.at[pl.ds(1, NP - 1)]
        return remote(group, group, sp_ss, sp_rs, dev_p(1))

    diagonal = lax.broadcasted_iota(jnp.int32, (ROWS, 128), 0) == lax.broadcasted_iota(jnp.int32, (ROWS, 128), 1)

    def return_block(i, h):
        if h == 0:
            copy_cr(i).wait_recv()
        for n in range(4):
            p = 4 * i + n
            sbr[h, p] = (do[i, h, n * ROWS : (n + 1) * ROWS, :] + dr[i, h, n].astype(F32)).astype(BF16)
            if p:
                copy_br(h, p).start()

    def side_block(i):
        for n in range(4):
            p = 4 * i + n
            row = jnp.sum(jnp.where(diagonal, side[p * ROWS : (p + 1) * ROWS, :], 0.0), axis=0, keepdims=True)
            sp[p] = jnp.broadcast_to(row, (8, 128))
            if p:
                copy_sp(p).start()

    for i in range(5):
        if i < 4:
            gelu_block(i)
            dx_block(i)
        if i > 0:
            return_block(i - 1, 0)
    for i in range(4):
        return_block(i, 1)
    for i in range(4):
        side_block(i)
    for h in range(2):
        late.append(lambda h=h: recv_br(h).wait_send())
    late.append(lambda: recv_sp().wait_send())

    def wide_in_body(n, _):
        at = pl.multiple_of((n // KC) * CW, CW)
        f = n % KC
        rows = rr[0, n // KC].reshape(NP * ROWS, CW)
        term = dot_tn(rows, dpre[f]).astype(BF16)
        grad_in[pl.ds(at, CW), pl.ds(pl.multiple_of(f * CW, CW), CW)] = term
        return 0

    def wide_out_body(n, _):
        f = n // KC
        k = n % KC
        rows = rr[1, k].reshape(NP * ROWS, CW)
        term = dot_tn(act[f], rows).astype(BF16)
        grad_out[pl.ds(pl.multiple_of(f * CW, CW), CW), pl.ds(pl.multiple_of(k * CW, CW), CW)] = term
        return 0

    for j in range(2):
        t = t_buf[j].astype(F32)
        t_all[j] = jnp.where(t != 0.0, 1.0, 0.0).T.astype(BF16)
        t_one[j, 0] = jnp.where(t > 0.0, 1.0, 0.0).astype(BF16)
        t_one[j, 1] = jnp.where(t < 0.0, 1.0, 0.0).astype(BF16)

    def copy_ar(h, j):
        return remote(sar.at[h, j], rar.at[h, (NZ - j) % NZ], ar_ss.at[h], ar_rs.at[h], dev_z(j))

    def recv_ar(h):
        group = rar.at[h, pl.ds(1, NZ - 1)]
        return remote(group, group, ar_ss.at[h], ar_rs.at[h], dev_z(1))

    def copy_sz(j):
        return remote(sz.at[j], sz_in.at[(NZ - j) % NZ], sz_ss, sz_rs, dev_z(j))

    def recv_sz():
        group = sz_in.at[pl.ds(1, NZ - 1)]
        return remote(group, group, sz_ss, sz_rs, dev_z(1))

    def stage_z(h):
        recv_br(h).wait_recv()
        for j in range(NQ):
            one = sbr if j == 0 else rbr
            yy[plane_of(j) % NQ] = (one[h, j].astype(F32) + rbr[h, twin(j)].astype(F32)).astype(BF16)
        sar[h] = dot_nn(swap[...], yy[...].reshape(ALL, CW)).astype(BF16).reshape(NZ, ROWS, CW)
        each(NZ, lambda j: copy_ar(h, j).start())
        rar[h, 0] = sar[h, 0]
        late.append(lambda: recv_ar(h).wait_send())

    lanes = lax.broadcasted_iota(jnp.int32, (ROWS, 128), 1)

    def side_z():
        recv_sp().wait_recv()
        for j in range(NQ):
            one = sp if j == 0 else sp_in
            row = (one[j] + sp_in[twin(j)])[0:1, :]
            s = jnp.sum(jnp.where(diagonal, jnp.broadcast_to(row, (ROWS, 128)), 0.0), axis=1, keepdims=True)
            hi = s.astype(BF16).astype(F32)
            ys[plane_of(j) % NQ] = jnp.where(lanes == 0, hi, jnp.where(lanes == 1, s - hi, 0.0)).astype(BF16)
        back = dot_nn(swap[...], ys[...].reshape(ALL, 128))
        for n in range(NZ):
            s = jnp.sum(back[n * ROWS : (n + 1) * ROWS, :], axis=1, keepdims=True)
            row = jnp.sum(jnp.where(diagonal, s, 0.0), axis=0, keepdims=True)
            sz[n] = jnp.broadcast_to(row, (8, 128))
        each(NZ, lambda j: copy_sz(j).start())
        sz_in[0] = sz[0]
        late.append(lambda: recv_sz().wait_send())

    stage_z(0)
    lax.fori_loop(0, KC * KC // 2, wide_in_body, 0)
    stage_z(1)
    side_z()
    lax.fori_loop(KC * KC // 2, KC * KC, wide_in_body, 0)
    out_in = pltpu.make_async_copy(grad_in, gin_hbm, o_sem.at[0])
    out_in.start()
    late.append(out_in.wait)
    pair(2, xg.at[other, other], xg.at[other, other]).wait_recv()
    pair(3, mixt.at[other], mixt.at[other]).wait_recv()

    def copy_p2(h, j):
        p = plane_of(j)
        return remote(
            rs_b.at[h, p // NQ, :, p % NQ], rs2.at[h, back(j)], p2_ss.at[h], p2_rs.at[h],
            dev_p(j),
        )

    def recv_p2(h):
        group = rs2.at[h, pl.ds(1, NP - 1)]
        return remote(group, group, p2_ss.at[h], p2_rs.at[h], dev_p(1))

    def mo_copy(h):
        return pair(4 + h, mo.at[h], mo_in.at[h])

    def home(h):
        recv_ar(h).wait_recv()
        rows = rar[h].reshape(ALL, CW)
        theirs = dot_nn(t_all[other], rows)
        ours = dot_nn(t_all[c], rows)
        mine = []
        for xhi in range(2):
            lane = slice(xhi * 128, (xhi + 1) * 128)
            mo[h, :, lane] = (xg[1, other, :, piece(xhi, c, h)].astype(F32) + theirs[:, lane]).astype(BF16)
            own = (xg[1, c, :, piece(xhi, c, h)].astype(F32) + ours[:, lane]).astype(BF16)
            mid[:, piece(xhi, c, h)] = own
            mine.append(own)
        mo_copy(h).start()
        late.append(mo_copy(h).wait_send)
        for xhi in range(2):
            lane = slice(xhi * 128, (xhi + 1) * 128)
            part = dot_nn(mixt[c], mine[xhi]) + dot_nn(mixt[other], mo[h, :, lane])
            rs_b[h, xhi] = part.astype(BF16).reshape(NZ, NQ, 16, 128)
        each(NP, lambda j: copy_p2(h, j).start())
        rs2[h, 0] = rs_b[h, xh, :, q]
        late.append(lambda: recv_p2(h).wait_send())

    home(0)
    lax.fori_loop(0, KC * KC // 2, wide_out_body, 0)
    home(1)
    lax.fori_loop(KC * KC // 2, KC * KC, wide_out_body, 0)
    out_out = pltpu.make_async_copy(grad_out, gout_hbm, o_sem.at[1])
    out_out.start()
    late.append(out_out.wait)

    for h in range(2):
        mo_copy(h).wait_recv()
        for xhi in range(2):
            mid[:, piece(xhi, other, h)] = mo_in[h, :, xhi * 128 : (xhi + 1) * 128]

    for n in range(4):
        rows = slice(n * CW, (n + 1) * CW)
        d_heads[:, rows] = dot_nt(mid[...], ap[rows, :]).astype(BF16)

    def backward(p, _):
        at = pl.ds(pl.multiple_of(p * 128, 128), 128)
        qp, kp, vp, gp = q_buf[:, at], k_buf[:, at], v_buf[:, at], d_heads[:, at]
        gq, gk, gv = [], [], []
        for n in range(2):
            prob = probs[2 * p + n]
            gv.append(dot_tn(prob.astype(BF16), gp))
            d_prob = dot_nt(masked(gp, n), vp)
            inner = jnp.sum(d_prob * prob, axis=1, keepdims=True)
            d_score = (prob * (d_prob - inner)).astype(BF16)
            gq.append(dot_nn(d_score, kp))
            gk.append(dot_tn(d_score, qp))
        grad_v[:, at] = jnp.where(left_lane, gv[0], gv[1]).astype(BF16)
        grad_q[:, at] = (jnp.where(left_lane, gq[0], gq[1]) * SCALE).astype(BF16)
        grad_k[:, at] = (jnp.where(left_lane, gk[0], gk[1]) * SCALE).astype(BF16)
        return 0

    lax.fori_loop(0, 4, backward, 0)

    for h in range(2):
        recv_p2(h).wait_recv()
        total = lax.fori_loop(1, NP, lambda j, t: t + rs2[h, j].astype(F32), rs2[h, 0].astype(F32))
        rs_c[:, :, h * 128 : (h + 1) * 128] = total.astype(BF16)

    def copy_p3(j):
        return remote(
            rs_c.at[(z + j) % NZ], rs3.at[(NZ - j) % NZ], p3_ss, p3_rs, dev_z(j)
        )

    def recv_p3():
        group = rs3.at[pl.ds(1, NZ - 1)]
        return remote(group, group, p3_ss, p3_rs, dev_z(1))

    each(NZ, lambda j: copy_p3(j).start())
    rs3[0] = rs_c[z]
    late.append(lambda: recv_p3().wait_send())

    recv_sz().wait_recv()
    row16 = lax.broadcasted_iota(jnp.int32, (16, 128), 0)

    def gate_terms(j):
        out = []
        for k in range(2):
            total = None
            for n in range(NZ):
                row = sz_in[n][0:1, :]
                hi = row.astype(BF16).astype(F32)
                both = jnp.where(row16 == 0, hi, jnp.where(row16 == 1, row - hi, 0.0)).astype(BF16)
                term = dot_nn(both[:, 0:ROWS], t_one[j, k, n * ROWS : (n + 1) * ROWS, :])
                total = term if total is None else total + term
            out.append(jnp.sum(total, axis=0, keepdims=True))
        return jnp.concatenate(out + [jnp.zeros((6, 128), F32)], axis=0)

    ga[...] = gate_terms(other)
    ga_copy = pair(6, ga, ga_in)
    ga_copy.start()
    late.append(ga_copy.wait_send)
    ours = gate_terms(c)
    lax.fori_loop(4, 8, backward, 0)
    ga_copy.wait_recv()
    for k in range(2):
        gates[k : k + 1, :] = (ours[k : k + 1, :] + ga_in[k : k + 1, :]) / gate[k]

    recv_p3().wait_recv()
    proj[...] = jnp.sum(rs3[...].astype(F32), axis=0).astype(BF16)

    for wait in late:
        wait()


def moe(lengths, ids, gate, x, g, q, k, v, ap, w_in, w_out):
    vmem = pl.BlockSpec(memory_space=pltpu.VMEM)
    smem = pl.BlockSpec(memory_space=pltpu.SMEM)
    hbm = pl.BlockSpec(memory_space=pl.ANY)
    V = pltpu.VMEM

    def dma(*shape):
        return [pltpu.SemaphoreType.DMA(shape)] * 2

    return pl.pallas_call(
        moe_kernel,
        out_shape=(
            *[jax.ShapeDtypeStruct((TOK, D), BF16)] * 4,
            jax.ShapeDtypeStruct((2, TOK), F32),
            jax.ShapeDtypeStruct((D, D), BF16),
            jax.ShapeDtypeStruct((D, D), BF16),
            jax.ShapeDtypeStruct((16, 256), BF16),
        ),
        in_specs=[smem, vmem, vmem] + [hbm] * 8,
        out_specs=(*[vmem] * 5, hbm, hbm, vmem),
        scratch_shapes=[
            V((TOK, D), BF16), V((TOK, D), BF16), V((TOK, D), BF16), V((D, D), BF16), V((16, TOK, TOK), F32), V((TOK, D), BF16),
            V((D, D), BF16), V((2, 2, 256, D), BF16), V((D, D), BF16), V((ALL, ALL), BF16), V((2, D, TOK), BF16),
            V((D, D), BF16), V((D, D), BF16), V((2, 2, TOK, D), BF16),
            V((2, ALL, TOK), BF16), V((2, ALL, TOK), BF16), V((2, TOK, ALL), BF16), V((2, 2, ALL, TOK), BF16),
            V((KC, NZ, ROWS, CW), BF16), V((KC, NZ, ROWS, CW), BF16), V((KC, NQ, ROWS, CW), BF16),
            V((2, KC, NP, ROWS, CW), BF16),
            V((4, BLK, D), F32), V((4, BLK, D), F32),
            V((KC, NP * ROWS, CW), BF16), V((KC, NP * ROWS, CW), BF16), V((NP * ROWS, 128), F32),
            V((4, 2, 4, ROWS, CW), BF16), V((4, 2, 4, ROWS, CW), BF16), V((4, 2, BLK, CW), F32),
            V((2, NP, ROWS, CW), BF16), V((2, NP, ROWS, CW), BF16),
            V((NQ, ROWS, CW), BF16), V((2, NZ, ROWS, CW), BF16), V((2, NZ, ROWS, CW), BF16),
            V((NP, 8, 128), F32), V((NP, 8, 128), F32), V((NQ, ROWS, 128), BF16),
            V((NZ, 8, 128), F32), V((NZ, 8, 128), F32), V((8, 128), F32), V((8, 128), F32),
            V((2, TOK, CW), BF16), V((2, TOK, CW), BF16),
            V((2, 2, NZ, NQ, 16, 128), BF16), V((2, NP, NZ, 16, 128), BF16),
            V((NZ, 16, 256), BF16), V((NZ, 16, 256), BF16),
            pltpu.SemaphoreType.DMA((8,)), pltpu.SemaphoreType.DMA((8,)), pltpu.SemaphoreType.DMA((2,)),
            *dma(7), *dma(KC), *dma(KC), *dma(KC), *dma(4),
            *dma(2), *dma(2), *dma(), *dma(), *dma(2), *dma(),
        ],
        compiler_params=pltpu.CompilerParams(
            collective_id=0, has_side_effects=True, vmem_limit_bytes=62 * 1024 * 1024
        ),
        cost_estimate=pl.CostEstimate(flops=14_000_000_000, bytes_accessed=12_000_000, transcendentals=1_310_720),
    )(lengths, ids, gate, x, g, q, k, v, ap, w_in, w_out)


def place_kernel(count, *refs):
    src, dst, held = refs[:count], refs[count : 2 * count], refs[2 * count : 3 * count]
    in_sem, out_sem = refs[3 * count :]
    loads, stores = [], []
    for n in range(count):
        rows = src[n].shape[0]
        pieces = 4 if rows == D else 1
        for m in range(pieces):
            at = pl.ds(m * (rows // pieces), rows // pieces)
            loads.append(pltpu.make_async_copy(src[n].at[at], held[n].at[at], in_sem.at[len(loads)]))
            stores.append(pltpu.make_async_copy(held[n].at[at], dst[n].at[at], out_sem.at[len(stores)]))
    for load in loads:
        load.start()
    for load, store in zip(loads, stores):
        load.wait()
        store.start()
    for store in stores:
        store.wait()


def place(arrays):
    hbm = pl.BlockSpec(memory_space=pl.ANY)
    count = len(arrays)
    return pl.pallas_call(
        functools.partial(place_kernel, count),
        out_shape=tuple(jax.ShapeDtypeStruct(a.shape, a.dtype) for a in arrays),
        in_specs=[hbm] * count,
        out_specs=(hbm,) * count,
        scratch_shapes=[pltpu.VMEM(a.shape, a.dtype) for a in arrays]
        + [pltpu.SemaphoreType.DMA((count + 6,)), pltpu.SemaphoreType.DMA((count + 6,))],
    )(*arrays)


def on_device(
    mid_acts, out_grad, queries, key_rows, value_head_rows, seq_lengths,
    expert_ids, gate_probs, wide_in, wide_out, attn_proj,
):
    results = moe(
        seq_lengths, expert_ids.T, gate_probs.T, mid_acts, out_grad, queries, key_rows, value_head_rows, attn_proj,
        wide_in[0], wide_out[0],
    )
    grad_mid, grad_q, grad_k, grad_v, grad_gates, grad_in, grad_out, proj = place(results)
    return (grad_mid, grad_q, grad_k, grad_v, grad_gates.T, grad_in[None], grad_out[None], proj)


def solution(mesh):
    both = ("expert", "replica")
    return jax.shard_map(
        on_device,
        mesh=mesh,
        in_specs=(
            P(both, None), P(both, None), P(both, None), P(both, None), P(both, None), P(both),
            P(both, None), P(both, None), P("expert", None, "replica"), P("expert", "replica", None), P(),
        ),
        out_specs=(
            P(both, None), P(both, None), P(both, None), P(both, None), P(both, None),
            P("expert", None, "replica"), P("expert", "replica", None), P("expert", "replica"),
        ),
        check_vma=False,
    )
```

```python
import functools
import math

import jax
import jax.numpy as jnp
from jax import lax
from jax.experimental import pallas as pl
from jax.experimental.pallas import tpu as pltpu
from jax.sharding import PartitionSpec as P

HEAD_SIZE = 64
GELU_C = 0.7978845608028654
GELU_A = 0.044715
MESH = pl.DeviceIdType.MESH

NZ, NQ, NP = 8, 8, 16
CAP = 5
TOK = 128
D = 1024
ROWS = 2 * NQ * CAP
ALL = NZ * ROWS
KC, CW = 4, 256
BLK = 4 * ROWS
F32 = jnp.float32
BF16 = jnp.bfloat16


def dot_nn(a, b):
    return jnp.dot(a, b, preferred_element_type=F32)


def dot_nt(a, b):
    return lax.dot_general(a, b, (((1,), (1,)), ((), ())), preferred_element_type=F32)


def dot_tn(a, b):
    return lax.dot_general(a, b, (((0,), (0,)), ((), ())), preferred_element_type=F32)


def moe_kernel(
    length, ids_ref, gate_ref, x_hbm, g_hbm, q_hbm, k_hbm, v_hbm, ap_hbm, w_in_hbm, w_out_hbm,
    mid, grad_q, grad_k, grad_v, gates, gin_hbm, gout_hbm, proj,
    q_buf, k_buf, v_buf, ap, probs, d_heads,
    w_in, w_arr, w_out, swap, mixt, grad_in, grad_out, xg, t_buf, t_use, t_all, t_one, sa, ra, sb, rr,
    pre, dact, act, dpre, xt, side, ds, dr, do, sbr, rbr, yy, sar, rar,
    sp, sp_in, ys, sz, sz_in, ga, ga_in, mo, mo_in, rs_b, rs2, rs_c, rs3,
    w_sem, n_sem, o_sem, pair_ss, pair_rs, a_ss, a_rs, b_ss, b_rs, c_ss, c_rs, cr_ss, cr_rs,
    br_ss, br_rs, ar_ss, ar_rs, sp_ss, sp_rs, sz_ss, sz_rs, p2_ss, p2_rs, p3_ss, p3_rs,
):
    e = lax.axis_index("expert")
    r = lax.axis_index("replica")
    z, q, xh, c = e // NQ, e % NQ, r // 2, r % 2
    other = 1 - c
    partner = (e, xh * 2 + other)
    late = []

    def dev_z(j):
        return (((z + j) % NZ) * NQ + q, r)

    def plane_of(j):
        i, n = j // 4, j % 4
        x = (xh * 2 + q // 4 + n) % 4
        return x // 2 * NQ + x % 2 * 4 + (q + n + i) % 4

    def back(j):
        return (4 - j // 4) % 4 * 4 + (4 - j % 4) % 4

    def twin(j):
        return (j // 4 + 2) % 4 * 4 + (j % 4 + 2) % 4

    def dev_p(j):
        p = plane_of(j)
        return (z * NQ + p % NQ, (p // NQ) * 2 + c)

    def remote(src, dst, ss, rs, dev):
        return pltpu.make_async_remote_copy(
            src_ref=src, dst_ref=dst, send_sem=ss, recv_sem=rs, device_id=dev, device_id_type=MESH
        )

    def pair(n, src, dst):
        return remote(src, dst, pair_ss.at[n], pair_rs.at[n], partner)

    def each(count, body):
        def step(j, _):
            body(j)
            return 0

        lax.fori_loop(1, count, step, 0)

    def piece(xhi, core, h):
        return pl.ds(pl.multiple_of(xhi * 512 + core * 256 + h * 128, 128), 128)

    tokens = [
        pltpu.make_async_copy(x_hbm, xg.at[0, c], w_sem.at[3]),
        pltpu.make_async_copy(g_hbm, xg.at[1, c], w_sem.at[4]),
    ]
    heads_in = [
        pltpu.make_async_copy(q_hbm, q_buf, w_sem.at[5]),
        pltpu.make_async_copy(k_hbm, k_buf, w_sem.at[6]),
        pltpu.make_async_copy(v_hbm, v_buf, w_sem.at[7]),
    ]
    loads = [
        pltpu.make_async_copy(w_in_hbm, w_in, w_sem.at[1]),
        pltpu.make_async_copy(w_out_hbm, w_out, w_sem.at[2]),
        pltpu.make_async_copy(ap_hbm, ap, w_sem.at[0]),
    ]
    arranged = []
    for n in range(8):
        core, h, xhi = n // 4, (n // 2) % 2, n % 2
        arranged.append(
            pltpu.make_async_copy(
                w_in_hbm.at[pl.ds(xhi * 512 + core * 256 + h * 128, 128)],
                w_arr.at[core, h, pl.ds(xhi * 128, 128)],
                n_sem.at[n],
            )
        )
    for copy in tokens + heads_in + loads + arranged:
        copy.start()

    bar = pltpu.get_barrier_semaphore()
    pl.semaphore_signal(bar, inc=1, device_id=partner, device_id_type=MESH)
    each(NZ, lambda j: pl.semaphore_signal(bar, inc=1, device_id=dev_z(j), device_id_type=MESH))
    each(NP, lambda j: pl.semaphore_signal(bar, inc=1, device_id=dev_p(j), device_id_type=MESH))

    above = lax.broadcasted_iota(jnp.int32, (TOK, TOK), 0)
    along = lax.broadcasted_iota(jnp.int32, (TOK, TOK), 1)

    def to_column(row):
        return jnp.sum(jnp.where(above == along, jnp.broadcast_to(row, (TOK, TOK)), 0), axis=1, keepdims=True)

    def count(which):
        return jnp.sum(jnp.where(which, 1, 0), axis=0, keepdims=True)

    ids = [ids_ref[k : k + 1, :] for k in range(2)]
    columns = [to_column(row) for row in ids]
    gate = [gate_ref[k : k + 1, :].astype(F32) for k in range(2)]
    slot = [
        count((columns[0] == ids[0]) & (above < along)),
        count(columns[0] == ids[1]) + count((columns[1] == ids[1]) & (above < along)),
    ]
    rows_of = lax.broadcasted_iota(jnp.int32, (ALL, TOK), 0)
    signed = None
    for k in range(2):
        place = ((ids[k] // NQ + NZ - z) % NZ) * ROWS + c * (NQ * CAP) + (ids[k] % NQ) * CAP + slot[k]
        place = jnp.where(slot[k] < CAP, place, -1)
        term = jnp.where(rows_of == place, gate[k] if k == 0 else -gate[k], 0.0)
        signed = term if signed is None else signed + term
    t_buf[c] = signed.astype(BF16)
    for copy in tokens:
        copy.wait()
    pl.semaphore_wait(bar, NZ + NP - 1)

    t_copy = pair(0, t_buf.at[c], t_buf.at[c])
    m_copy = pair(1, xg.at[other, c], xg.at[other, c])
    n_copy = pair(2, xg.at[c, c], xg.at[c, c])
    t_copy.start()
    m_copy.start()
    n_copy.start()
    late.extend([t_copy.wait_send, m_copy.wait_send, n_copy.wait_send])
    t_copy.wait_recv()
    for j in range(2):
        size = jnp.abs(t_buf[j].astype(F32))
        t_use[j] = jnp.where(c == 0, jnp.where(size > 0.0, 1.0, 0.0), size).astype(BF16)
    pair(1, xg.at[c, other], xg.at[c, other]).wait_recv()

    def copy_a(k, j):
        return remote(sa.at[k, j], ra.at[k, (NZ - j) % NZ], a_ss.at[k], a_rs.at[k], dev_z(j))

    def recv_a(k):
        group = ra.at[k, pl.ds(1, NZ - 1)]
        return remote(group, group, a_ss.at[k], a_rs.at[k], dev_z(1))

    def copy_b(k, j):
        return remote(
            sb.at[k, plane_of(j) % NQ], rr.at[c, k, back(j)], b_ss.at[k], b_rs.at[k], dev_p(j)
        )

    def recv_b(k):
        group = rr.at[c, k, pl.ds(1, NP - 1)]
        return remote(group, group, b_ss.at[k], b_rs.at[k], dev_p(1))

    def copy_c(k):
        return remote(rr.at[c, k], rr.at[c, k], c_ss.at[k], c_rs.at[k], partner)

    def recv_c(k):
        return remote(rr.at[other, k], rr.at[other, k], c_ss.at[k], c_rs.at[k], partner)

    def stage_a(k):
        each(NZ, lambda j: copy_a(k, j).start())
        ra[k, 0] = sa[k, 0]

    AHEAD = 2
    for k in range(KC):
        cols = slice(k * CW, (k + 1) * CW)
        rows = dot_nn(t_use[0], xg[c, 0, :, cols]) + dot_nn(t_use[1], xg[c, 1, :, cols])
        sa[k] = rows.astype(BF16).reshape(NZ, ROWS, CW)
        if k < AHEAD:
            stage_a(k)
    left_lane = lax.broadcasted_iota(jnp.int32, (TOK, 128), 1) < HEAD_SIZE
    live = lax.broadcasted_iota(jnp.int32, (TOK, TOK), 1) < length[0]
    SCALE = 1.0 / math.sqrt(HEAD_SIZE)

    def masked(block, n):
        block = block.astype(F32)
        return (jnp.where(left_lane, block, 0.0) if n == 0 else jnp.where(left_lane, 0.0, block)).astype(BF16)

    def forward(p, _):
        at = pl.ds(pl.multiple_of(p * 128, 128), 128)
        qp, kp, vp = q_buf[:, at], k_buf[:, at], v_buf[:, at]
        out = []
        for n in range(2):
            scores = jnp.where(live, dot_nt(masked(qp, n), kp) * SCALE, -1000000000.0)
            expo = jnp.exp(scores - jnp.max(scores, axis=1, keepdims=True))
            prob = expo / jnp.sum(expo, axis=1, keepdims=True)
            probs[2 * p + n] = prob
            out.append(dot_nn(prob.astype(BF16), vp))
        mixt[c, at, :] = jnp.where(left_lane, out[0], out[1]).T.astype(BF16)
        return 0

    for copy in heads_in:
        copy.wait()
    lax.fori_loop(0, 3, forward, 0)

    row = lax.broadcasted_iota(jnp.int32, (8, ALL), 1)
    place = (row % (NQ * CAP)) // CAP * ROWS + (row % ROWS) // (NQ * CAP) * (NQ * CAP) + row // ROWS * CAP + row % CAP
    for n in range(8):
        rows = lax.broadcasted_iota(jnp.int32, (ROWS, ALL), 0) + n * ROWS
        swap[n * ROWS : (n + 1) * ROWS, :] = jnp.where(rows == place[0:1, :], 1.0, 0.0).astype(BF16)

    def stage_b(k):
        recv_a(k).wait_recv()
        if k + AHEAD < KC:
            stage_a(k + AHEAD)
        rows = dot_nn(swap[...], ra[k].reshape(ALL, CW))
        sb[k] = rows.astype(BF16).reshape(NQ, ROWS, CW)
        each(NP, lambda j: copy_b(k, j).start())
        rr[c, k, 0] = sb[k, q]

    def stage_c(k):
        recv_b(k).wait_recv()
        copy_c(k).start()

    def stage_d(k):
        recv_c(k).wait_recv()
        if k == 0:
            loads[0].wait()
            loads[1].wait()

        if k < KC - 1:
            lax.fori_loop(0, 4, lambda i, _: d_block(k, i), 0)
            xt[k] = rr[0, k].reshape(NP * ROWS, CW).T

    def d_block(k, i):
        xk = rr[0, k, pl.ds(4 * i, 4)].reshape(BLK, CW)
        gk = rr[1, k, pl.ds(4 * i, 4)].reshape(BLK, CW)
        p_new = dot_nn(xk, w_in[k * CW : (k + 1) * CW, :])
        d_new = dot_nt(gk, w_out[:, k * CW : (k + 1) * CW])
        if k == 0:
            pre[i] = p_new
            dact[i] = d_new
        else:
            pre[i] += p_new
            dact[i] += d_new
        return 0

    for step in range(KC + 2):
        if step < KC:
            stage_b(step)
        if step in (1, 2):
            lax.fori_loop(2 * step + 1, 2 * step + 3, forward, 0)
        if step == 3:
            forward(7, 0)
            x_copy = pair(3, mixt.at[c], mixt.at[c])
            x_copy.start()
            late.append(x_copy.wait_send)
        if 0 <= step - 1 < KC:
            stage_c(step - 1)
        if 0 <= step - 2 < KC:
            stage_d(step - 2)
        if step == 1:
            loads[2].wait()
            for copy in arranged:
                copy.wait()
    for k in range(KC):
        late.append(lambda k=k: recv_a(k).wait_send())
        late.append(lambda k=k: recv_b(k).wait_send())
        late.append(copy_c(k).wait_send)

    SUB = 32

    def gelu_block(i):
        def body(n, _):
            at = pl.multiple_of(n * SUB, SUB)
            u = pre[i, pl.ds(at, SUB), :]
            da = dact[i, pl.ds(at, SUB), :]
            uu = u * u
            inner = jnp.tanh(GELU_C * (u + GELU_A * uu * u))
            half = 0.5 * (1.0 + inner)
            a = (u * half).astype(BF16)
            slope = half + 0.5 * u * (1.0 - inner * inner) * (GELU_C + (3.0 * GELU_A * GELU_C) * uu)
            dp = (da * slope).astype(BF16)
            s = jnp.sum(a.astype(F32) * da, axis=1, keepdims=True)
            to = pl.multiple_of(i * BLK + at, SUB)
            side[pl.ds(to, SUB), :] = jnp.broadcast_to(s, (SUB, 128))
            for f in range(KC):
                act[f, pl.ds(to, SUB), :] = a[:, f * CW : (f + 1) * CW]
                dpre[f, pl.ds(to, SUB), :] = dp[:, f * CW : (f + 1) * CW]
            return 0

        lax.fori_loop(0, BLK // SUB, body, 0)

    def copy_cr(i):
        return remote(ds.at[i], dr.at[i], cr_ss.at[i], cr_rs.at[i], partner)

    def dx_block(i):
        def part(core, h):
            total = None
            for f in range(KC):
                term = dot_nt(dpre[f, i * BLK : (i + 1) * BLK, :], w_arr[core, h, :, f * CW : (f + 1) * CW])
                total = term if total is None else total + term
            return total

        for h in range(2):
            ds[i, h] = part(other, h).astype(BF16).reshape(4, ROWS, CW)
        copy_cr(i).start()
        late.append(copy_cr(i).wait_send)
        for h in range(2):
            do[i, h] = part(c, h)

    def copy_br(h, j):
        return remote(sbr.at[h, j], rbr.at[h, back(j)], br_ss.at[h], br_rs.at[h], dev_p(j))

    def recv_br(h):
        group = rbr.at[h, pl.ds(1, NP - 1)]
        return remote(group, group, br_ss.at[h], br_rs.at[h], dev_p(1))

    def copy_sp(j):
        return remote(sp.at[j], sp_in.at[back(j)], sp_ss, sp_rs, dev_p(j))

    def recv_sp():
        group = sp_in.at[pl.ds(1, NP - 1)]
        return remote(group, group, sp_ss, sp_rs, dev_p(1))

    diagonal = lax.broadcasted_iota(jnp.int32, (ROWS, 128), 0) == lax.broadcasted_iota(jnp.int32, (ROWS, 128), 1)

    def return_block(i, h):
        if h == 0:
            copy_cr(i).wait_recv()
        for n in range(4):
            p = 4 * i + n
            sbr[h, p] = (do[i, h, n * ROWS : (n + 1) * ROWS, :] + dr[i, h, n].astype(F32)).astype(BF16)
            if p:
                copy_br(h, p).start()

    def side_block(i):
        for n in range(4):
            p = 4 * i + n
            row = jnp.sum(jnp.where(diagonal, side[p * ROWS : (p + 1) * ROWS, :], 0.0), axis=0, keepdims=True)
            sp[p] = jnp.broadcast_to(row, (8, 128))
            if p:
                copy_sp(p).start()

    for i in range(5):
        if i < 4:
            d_block(KC - 1, i)
            gelu_block(i)
            dx_block(i)
        if i > 0:
            return_block(i - 1, 0)
    for i in range(4):
        return_block(i, 1)
    for h in range(2):
        late.append(lambda h=h: recv_br(h).wait_send())
    late.append(lambda: recv_sp().wait_send())

    def wide_in_body(k, _):
        at = pl.multiple_of(k * CW, CW)
        for f in range(KC):
            grad_in[pl.ds(at, CW), f * CW : (f + 1) * CW] = dot_nn(xt[k], dpre[f]).astype(BF16)
        return 0

    def wide_out_body(f, _):
        at = pl.multiple_of(f * CW, CW)
        rows = act[f].T
        for k in range(KC):
            term = dot_nn(rows, rr[1, k].reshape(NP * ROWS, CW)).astype(BF16)
            grad_out[pl.ds(at, CW), k * CW : (k + 1) * CW] = term
        return 0

    for j in range(2):
        t = t_buf[j].astype(F32)
        t_all[j] = jnp.where(t != 0.0, 1.0, 0.0).T.astype(BF16)
        t_one[j, 0] = jnp.where(t > 0.0, 1.0, 0.0).astype(BF16)
        t_one[j, 1] = jnp.where(t < 0.0, 1.0, 0.0).astype(BF16)

    def copy_ar(h, j):
        return remote(sar.at[h, j], rar.at[h, (NZ - j) % NZ], ar_ss.at[h], ar_rs.at[h], dev_z(j))

    def recv_ar(h):
        group = rar.at[h, pl.ds(1, NZ - 1)]
        return remote(group, group, ar_ss.at[h], ar_rs.at[h], dev_z(1))

    def copy_sz(j):
        return remote(sz.at[j], sz_in.at[(NZ - j) % NZ], sz_ss, sz_rs, dev_z(j))

    def recv_sz():
        group = sz_in.at[pl.ds(1, NZ - 1)]
        return remote(group, group, sz_ss, sz_rs, dev_z(1))

    def stage_z(h):
        recv_br(h).wait_recv()
        for j in range(NQ):
            one = sbr if j == 0 else rbr
            yy[plane_of(j) % NQ] = (one[h, j].astype(F32) + rbr[h, twin(j)].astype(F32)).astype(BF16)
        sar[h] = dot_nn(swap[...], yy[...].reshape(ALL, CW)).astype(BF16).reshape(NZ, ROWS, CW)
        each(NZ, lambda j: copy_ar(h, j).start())
        rar[h, 0] = sar[h, 0]
        late.append(lambda: recv_ar(h).wait_send())

    lanes = lax.broadcasted_iota(jnp.int32, (ROWS, 128), 1)

    def side_z():
        recv_sp().wait_recv()
        for j in range(NQ):
            one = sp if j == 0 else sp_in
            row = (one[j] + sp_in[twin(j)])[0:1, :]
            s = jnp.sum(jnp.where(diagonal, jnp.broadcast_to(row, (ROWS, 128)), 0.0), axis=1, keepdims=True)
            hi = s.astype(BF16).astype(F32)
            ys[plane_of(j) % NQ] = jnp.where(lanes == 0, hi, jnp.where(lanes == 1, s - hi, 0.0)).astype(BF16)
        back = dot_nn(swap[...], ys[...].reshape(ALL, 128))
        for n in range(NZ):
            s = jnp.sum(back[n * ROWS : (n + 1) * ROWS, :], axis=1, keepdims=True)
            row = jnp.sum(jnp.where(diagonal, s, 0.0), axis=0, keepdims=True)
            sz[n] = jnp.broadcast_to(row, (8, 128))
        each(NZ, lambda j: copy_sz(j).start())
        sz_in[0] = sz[0]
        late.append(lambda: recv_sz().wait_send())

    stage_z(0)
    for i in range(4):
        side_block(i)
    lax.fori_loop(0, 2, wide_in_body, 0)
    stage_z(1)
    side_z()
    xt[3] = rr[0, 3].reshape(NP * ROWS, CW).T
    lax.fori_loop(2, 4, wide_in_body, 0)
    out_in = pltpu.make_async_copy(grad_in, gin_hbm, o_sem.at[0])
    out_in.start()
    late.append(out_in.wait)
    pair(2, xg.at[other, other], xg.at[other, other]).wait_recv()
    pair(3, mixt.at[other], mixt.at[other]).wait_recv()

    def copy_p2(h, j):
        p = plane_of(j)
        return remote(
            rs_b.at[h, p // NQ, :, p % NQ], rs2.at[h, back(j)], p2_ss.at[h], p2_rs.at[h],
            dev_p(j),
        )

    def recv_p2(h):
        group = rs2.at[h, pl.ds(1, NP - 1)]
        return remote(group, group, p2_ss.at[h], p2_rs.at[h], dev_p(1))

    def mo_copy(h):
        return pair(4 + h, mo.at[h], mo_in.at[h])

    def home(h):
        recv_ar(h).wait_recv()
        rows = rar[h].reshape(ALL, CW)
        theirs = dot_nn(t_all[other], rows)
        ours = dot_nn(t_all[c], rows)
        mine = []
        for xhi in range(2):
            lane = slice(xhi * 128, (xhi + 1) * 128)
            mo[h, :, lane] = (xg[1, other, :, piece(xhi, c, h)].astype(F32) + theirs[:, lane]).astype(BF16)
            own = (xg[1, c, :, piece(xhi, c, h)].astype(F32) + ours[:, lane]).astype(BF16)
            mid[:, piece(xhi, c, h)] = own
            mine.append(own)
        mo_copy(h).start()
        late.append(mo_copy(h).wait_send)
        for xhi in range(2):
            lane = slice(xhi * 128, (xhi + 1) * 128)
            part = dot_nn(mixt[c], mine[xhi]) + dot_nn(mixt[other], mo[h, :, lane])
            rs_b[h, xhi] = part.astype(BF16).reshape(NZ, NQ, 16, 128)
        each(NP, lambda j: copy_p2(h, j).start())
        rs2[h, 0] = rs_b[h, xh, :, q]
        late.append(lambda: recv_p2(h).wait_send())

    home(0)
    lax.fori_loop(0, 2, wide_out_body, 0)
    home(1)
    lax.fori_loop(2, 4, wide_out_body, 0)
    out_out = pltpu.make_async_copy(grad_out, gout_hbm, o_sem.at[1])
    out_out.start()
    late.append(out_out.wait)

    for h in range(2):
        mo_copy(h).wait_recv()
        for xhi in range(2):
            mid[:, piece(xhi, other, h)] = mo_in[h, :, xhi * 128 : (xhi + 1) * 128]

    for n in range(4):
        rows = slice(n * CW, (n + 1) * CW)
        d_heads[:, rows] = dot_nt(mid[...], ap[rows, :]).astype(BF16)

    def backward(p, _):
        at = pl.ds(pl.multiple_of(p * 128, 128), 128)
        qp, kp, vp, gp = q_buf[:, at], k_buf[:, at], v_buf[:, at], d_heads[:, at]
        gq, gk, gv = [], [], []
        for n in range(2):
            prob = probs[2 * p + n]
            gv.append(dot_tn(prob.astype(BF16), gp))
            d_prob = dot_nt(masked(gp, n), vp)
            inner = jnp.sum(d_prob * prob, axis=1, keepdims=True)
            d_score = (prob * (d_prob - inner)).astype(BF16)
            gq.append(dot_nn(d_score, kp))
            gk.append(dot_tn(d_score, qp))
        grad_v[:, at] = jnp.where(left_lane, gv[0], gv[1]).astype(BF16)
        grad_q[:, at] = (jnp.where(left_lane, gq[0], gq[1]) * SCALE).astype(BF16)
        grad_k[:, at] = (jnp.where(left_lane, gk[0], gk[1]) * SCALE).astype(BF16)
        return 0

    lax.fori_loop(0, 4, backward, 0)

    for h in range(2):
        recv_p2(h).wait_recv()
        total = lax.fori_loop(1, NP, lambda j, t: t + rs2[h, j].astype(F32), rs2[h, 0].astype(F32))
        rs_c[:, :, h * 128 : (h + 1) * 128] = total.astype(BF16)

    def copy_p3(j):
        return remote(
            rs_c.at[(z + j) % NZ], rs3.at[(NZ - j) % NZ], p3_ss, p3_rs, dev_z(j)
        )

    def recv_p3():
        group = rs3.at[pl.ds(1, NZ - 1)]
        return remote(group, group, p3_ss, p3_rs, dev_z(1))

    each(NZ, lambda j: copy_p3(j).start())
    rs3[0] = rs_c[z]
    late.append(lambda: recv_p3().wait_send())

    recv_sz().wait_recv()
    row16 = lax.broadcasted_iota(jnp.int32, (16, 128), 0)

    def gate_terms(j):
        out = []
        for k in range(2):
            total = None
            for n in range(NZ):
                row = sz_in[n][0:1, :]
                hi = row.astype(BF16).astype(F32)
                both = jnp.where(row16 == 0, hi, jnp.where(row16 == 1, row - hi, 0.0)).astype(BF16)
                term = dot_nn(both[:, 0:ROWS], t_one[j, k, n * ROWS : (n + 1) * ROWS, :])
                total = term if total is None else total + term
            out.append(jnp.sum(total, axis=0, keepdims=True))
        return jnp.concatenate(out + [jnp.zeros((6, 128), F32)], axis=0)

    ga[...] = gate_terms(other)
    ga_copy = pair(6, ga, ga_in)
    ga_copy.start()
    late.append(ga_copy.wait_send)
    ours = gate_terms(c)
    lax.fori_loop(4, 8, backward, 0)
    ga_copy.wait_recv()
    for k in range(2):
        gates[k : k + 1, :] = (ours[k : k + 1, :] + ga_in[k : k + 1, :]) / gate[k]

    recv_p3().wait_recv()
    proj[...] = jnp.sum(rs3[...].astype(F32), axis=0).astype(BF16)

    for wait in late:
        wait()


def moe(lengths, ids, gate, x, g, q, k, v, ap, w_in, w_out):
    vmem = pl.BlockSpec(memory_space=pltpu.VMEM)
    smem = pl.BlockSpec(memory_space=pltpu.SMEM)
    hbm = pl.BlockSpec(memory_space=pl.ANY)
    V = pltpu.VMEM

    def dma(*shape):
        return [pltpu.SemaphoreType.DMA(shape)] * 2

    return pl.pallas_call(
        moe_kernel,
        out_shape=(
            *[jax.ShapeDtypeStruct((TOK, D), BF16)] * 4,
            jax.ShapeDtypeStruct((2, TOK), F32),
            jax.ShapeDtypeStruct((D, D), BF16),
            jax.ShapeDtypeStruct((D, D), BF16),
            jax.ShapeDtypeStruct((16, 256), BF16),
        ),
        in_specs=[smem, vmem, vmem] + [hbm] * 8,
        out_specs=(*[vmem] * 5, hbm, hbm, vmem),
        scratch_shapes=[
            V((TOK, D), BF16), V((TOK, D), BF16), V((TOK, D), BF16), V((D, D), BF16), V((16, TOK, TOK), F32), V((TOK, D), BF16),
            V((D, D), BF16), V((2, 2, 256, D), BF16), V((D, D), BF16), V((ALL, ALL), BF16), V((2, D, TOK), BF16),
            V((D, D), BF16), V((D, D), BF16), V((2, 2, TOK, D), BF16),
            V((2, ALL, TOK), BF16), V((2, ALL, TOK), BF16), V((2, TOK, ALL), BF16), V((2, 2, ALL, TOK), BF16),
            V((KC, NZ, ROWS, CW), BF16), V((KC, NZ, ROWS, CW), BF16), V((KC, NQ, ROWS, CW), BF16),
            V((2, KC, NP, ROWS, CW), BF16),
            V((4, BLK, D), F32), V((4, BLK, D), F32),
            V((KC, NP * ROWS, CW), BF16), V((KC, NP * ROWS, CW), BF16), V((KC, CW, NP * ROWS), BF16), V((NP * ROWS, 128), F32),
            V((4, 2, 4, ROWS, CW), BF16), V((4, 2, 4, ROWS, CW), BF16), V((4, 2, BLK, CW), F32),
            V((2, NP, ROWS, CW), BF16), V((2, NP, ROWS, CW), BF16),
            V((NQ, ROWS, CW), BF16), V((2, NZ, ROWS, CW), BF16), V((2, NZ, ROWS, CW), BF16),
            V((NP, 8, 128), F32), V((NP, 8, 128), F32), V((NQ, ROWS, 128), BF16),
            V((NZ, 8, 128), F32), V((NZ, 8, 128), F32), V((8, 128), F32), V((8, 128), F32),
            V((2, TOK, CW), BF16), V((2, TOK, CW), BF16),
            V((2, 2, NZ, NQ, 16, 128), BF16), V((2, NP, NZ, 16, 128), BF16),
            V((NZ, 16, 256), BF16), V((NZ, 16, 256), BF16),
            pltpu.SemaphoreType.DMA((8,)), pltpu.SemaphoreType.DMA((8,)), pltpu.SemaphoreType.DMA((2,)),
            *dma(7), *dma(KC), *dma(KC), *dma(KC), *dma(4),
            *dma(2), *dma(2), *dma(), *dma(), *dma(2), *dma(),
        ],
        compiler_params=pltpu.CompilerParams(
            collective_id=0, has_side_effects=True, vmem_limit_bytes=62 * 1024 * 1024
        ),
        cost_estimate=pl.CostEstimate(flops=14_000_000_000, bytes_accessed=12_000_000, transcendentals=1_310_720),
    )(lengths, ids, gate, x, g, q, k, v, ap, w_in, w_out)


def place_kernel(count, *refs):
    src, dst, held = refs[:count], refs[count : 2 * count], refs[2 * count : 3 * count]
    in_sem, out_sem = refs[3 * count :]
    loads, stores = [], []
    for n in range(count):
        rows = src[n].shape[0]
        pieces = 4 if rows == D else 1
        for m in range(pieces):
            at = pl.ds(m * (rows // pieces), rows // pieces)
            loads.append(pltpu.make_async_copy(src[n].at[at], held[n].at[at], in_sem.at[len(loads)]))
            stores.append(pltpu.make_async_copy(held[n].at[at], dst[n].at[at], out_sem.at[len(stores)]))
    for load in loads:
        load.start()
    for load, store in zip(loads, stores):
        load.wait()
        store.start()
    for store in stores:
        store.wait()


def place(arrays):
    hbm = pl.BlockSpec(memory_space=pl.ANY)
    count = len(arrays)
    return pl.pallas_call(
        functools.partial(place_kernel, count),
        out_shape=tuple(jax.ShapeDtypeStruct(a.shape, a.dtype) for a in arrays),
        in_specs=[hbm] * count,
        out_specs=(hbm,) * count,
        scratch_shapes=[pltpu.VMEM(a.shape, a.dtype) for a in arrays]
        + [pltpu.SemaphoreType.DMA((count + 6,)), pltpu.SemaphoreType.DMA((count + 6,))],
    )(*arrays)


def on_device(
    mid_acts, out_grad, queries, key_rows, value_head_rows, seq_lengths,
    expert_ids, gate_probs, wide_in, wide_out, attn_proj,
):
    results = moe(
        seq_lengths, expert_ids.T, gate_probs.T, mid_acts, out_grad, queries, key_rows, value_head_rows, attn_proj,
        wide_in[0], wide_out[0],
    )
    grad_mid, grad_q, grad_k, grad_v, grad_gates, grad_in, grad_out, proj = place(results)
    return (grad_mid, grad_q, grad_k, grad_v, grad_gates.T, grad_in[None], grad_out[None], proj)


def solution(mesh):
    both = ("expert", "replica")
    return jax.shard_map(
        on_device,
        mesh=mesh,
        in_specs=(
            P(both, None), P(both, None), P(both, None), P(both, None), P(both, None), P(both),
            P(both, None), P(both, None), P("expert", None, "replica"), P("expert", "replica", None), P(),
        ),
        out_specs=(
            P(both, None), P(both, None), P(both, None), P(both, None), P(both, None),
            P("expert", None, "replica"), P("expert", "replica", None), P("expert", "replica"),
        ),
        check_vma=False,
    )
```
